256 devices in a mesh: dp: 4 (over z_lo, core), expert: 16 (over y, z_hi), tensor: 4 (over x).
Axes of the slice: x: 4, y: 4, z: 8 (z_hi: 4, z_lo: 2; z = z_hi * 2 + z_lo), core: 2. Of those that a mesh axis runs over, the one named last changes fastest.
Arguments:
- master: float32 [64, 2048, 1024], P('expert', ('dp', 'tensor')), may hold values from -0.125 to 0.125
- first_moment: float32 [64, 2048, 1024], P('expert', ('dp', 'tensor')), may hold values from -0.03 to 0.03
- second_moment: float32 [64, 2048, 1024], P('expert', ('dp', 'tensor')), may hold values from 1e-05 to 0.001
- gradient: bfloat16 [64, 2048, 1024], P('expert', ('dp', 'tensor')), may hold values from -0.119628906 to 0.119628906
- tokens: bfloat16 [2, 8192, 2048], P(None, ('dp', 'expert')), may hold values from -6 to 6
- expert_ids: int32 [2, 8192, 8], P(None, ('dp', 'expert')), may hold values from 0 to 63, all different within a row; in each aligned block of 128 rows (0 to 127, 128 to 255, ..., all dimensions but the last counted through in order) at most 32 rows name the same one
- router_scores: float32 [2, 8192, 8], P(None, ('dp', 'expert')), may hold values from 0.1 to 1
Outputs:
- new_master: float32 [64, 2048, 1024], P('expert', ('dp', 'tensor'))
- mixed: bfloat16 [2, 8192, 1024], P(None, ('dp', 'expert'), 'tensor')
The draws below stay inside these ranges and needn't reach their ends.
Inputs may be any that keep to these rules, and one draw needn't show every extreme that they name: `expert_ids`: each token names 8 different experts. Within the tokens of one step that lie on one token group (aligned blocks of 128 rows), no expert is named more than 32 times, a bound that some block reaches.
All inputs are finite; a program needn't handle non-finite values.
Results may differ from the reference program's by a relative error of at most 0.0053.
Values may be sent and summed in bfloat16 or wider, within the bound.
No kernel may reach another device: no remote copies, remote signals or barrier semaphores. Data moves between devices by JAX's collectives and lax.ppermute only.
A program may use at most 128 MiB of HBM per device.

```python
import math
import jax
import jax.numpy as jnp
import numpy as np
from jax import lax

D = 2048
F = 1024
TOPK = 8
STEPS = 2
TOK_DEV = 128
EXPERTS = 64
TOKENS = 8192
CAP = 32
N_DP = 4
N_EXPERT = 16


def shard_levels(key, dims, shards, least, top_value):
    loudness = 1.0
    for dim, blocks in shards:
        steps = jax.random.uniform(jax.random.fold_in(jax.random.fold_in(key, 6), dim), (blocks,), jnp.float32, least / len(shards), top_value / len(shards))
        loudness = loudness * jnp.repeat(jnp.exp(steps), dims[dim] // blocks).reshape((-1,) + (1,) * (len(dims) - 1 - dim))
    return loudness


def shared_out(stream_key, own, number, rows, count, top, reach, lean):
    order = jax.random.permutation(stream_key, count)
    crowded, ordinary = load_shares(count, rows * top, reach, lean, True), load_shares(count, rows * top, reach, lean, False)
    places = jnp.arange(count)

    def named(tallies, offset_by):
        used = int((tallies > 0).sum())
        fixed = max(1, used // 4)
        moved = fixed + (places - fixed + offset_by * (used - fixed)) % max(1, count - fixed)
        return jnp.zeros((count,), jnp.int32).at[order[jnp.where(places < fixed, places, moved)]].set(jnp.asarray(tallies, jnp.int32))

    tallies = jnp.where(number % 4 == 0, named(crowded, number // 4), named(ordinary, number - number // 4 - 1))
    mixed = jax.random.permutation(jax.random.fold_in(own, 3), count)
    source_of, sink = mixed[0:count // 2 * 2:2], mixed[1:count // 2 * 2:2]
    slack = jnp.minimum(tallies[source_of] - 1, reach - tallies[sink]) // 2
    slack = jnp.where((source_of == order[0]) | (sink == order[0]) | (tallies[sink] == 0), 0, jnp.maximum(slack, 0))
    moved = jax.random.randint(jax.random.fold_in(own, 4), (count // 2,), 0, 1 << 20) % (slack + 1)
    tallies = tallies.at[source_of].add(-moved).at[sink].add(moved)
    members = jnp.searchsorted(jnp.cumsum(tallies), jnp.arange(rows * top), side="right").astype(jnp.int32)
    grid = members.reshape(top, rows).T
    grid = grid[jax.random.permutation(jax.random.fold_in(own, 1), rows)]
    offset_by = jax.random.randint(jax.random.fold_in(own, 2), (rows, 1), 0, top)
    return jnp.take_along_axis(grid, (jnp.arange(top)[None, :] + offset_by) % top, axis=1)


def load_shares(count, total, bound, lean, full):
    weights = [(1 << 20) // math.isqrt(standing ** lean) + 1 for standing in range(1, count + 1)]
    largest = bound if full else min(bound, max(-(-total // count), total * weights[0] // sum(weights)))
    least = 1 if total - largest >= count - 1 else 0
    counts, rest = [largest] + [least] * (count - 1), total - largest - least * (count - 1)
    while rest > 0:
        movable = [i for i in range(1, count) if counts[i] < largest] or [i for i in range(1, count) if counts[i] < bound]
        pool, budget = sum([weights[i] for i in movable]), rest
        for i in movable:
            addition = min(bound - counts[i], max(1, budget * weights[i] // pool), rest)
            counts[i] = counts[i] + addition
            rest = rest - addition
    return np.array(counts)


def bell_draw(stream_key, extent, deviation, most, split=(), held_as=jnp.bfloat16):
    drawn = jax.random.normal(stream_key, extent, jnp.float32) * deviation
    if len(split) > 0:
        drawn = shard_levels(stream_key, extent, split, -0.22, 0.18) * drawn
    return jnp.clip(drawn, min=-most, max=most).astype(held_as)


def setup_inputs(seed: int = 0) -> dict:
    key_of = jax.random.split(jax.random.key(seed), 8)
    master = bell_draw(key_of[0], (EXPERTS, D, F), D ** -0.5, 0.125, ((0, 16), (1, 16)), jnp.float32)
    first_moment = bell_draw(key_of[1], (EXPERTS, D, F), 0.005, 0.03, ((0, 16), (1, 16)), jnp.float32)
    second_moment = jnp.clip(jnp.exp(math.log(0.001) - 4.6051703 * jax.random.uniform(key_of[2], (EXPERTS, D, F), jnp.float32) ** shard_levels(key_of[2], (EXPERTS, D, F), ((0, 16), (1, 16)), -0.2, 0.2)), 9.999999747378752e-06, 0.001)
    gradient = bell_draw(key_of[3], (EXPERTS, D, F), 0.02, 0.119628906, ((0, 16), (1, 16)))
    tokens = bell_draw(key_of[4], (STEPS, TOKENS, D), 1.0, 6.0, ((1, 64),))
    expert_ids_keys = jax.random.split(jax.random.fold_in(key_of[5], 1), STEPS * TOKENS // TOK_DEV)
    expert_ids_turns = jax.random.permutation(jax.random.fold_in(key_of[5], 3), STEPS * TOKENS // TOK_DEV)
    expert_ids = jax.vmap(lambda own, number: shared_out(jax.random.fold_in(key_of[5], 2), own, number, TOK_DEV, EXPERTS, TOPK, CAP, 2))(expert_ids_keys, expert_ids_turns).reshape((STEPS, TOKENS, TOPK))
    router_scores = jnp.clip(jnp.exp(math.log(1.0) - 2.3025851 * jax.random.uniform(key_of[6], (STEPS, TOKENS, TOPK), jnp.float32) ** shard_levels(key_of[6], (STEPS, TOKENS, TOPK), ((1, 64),), -0.2, 0.2)), 0.1, 1.0)
    return dict(master=master, first_moment=first_moment, second_moment=second_moment, gradient=gradient, tokens=tokens, expert_ids=expert_ids, router_scores=router_scores)


learn_rate = 0.01
decay_rate = 0.1
beta_one = 0.9
beta_two = 0.95
epsilon = 1e-08
correct_one = 1.0 - 0.9 ** 4
correct_two = 1.0 - 0.95 ** 4

def adam_update(master, first_moment, second_moment, gradient):
    grad_full = gradient.astype(jnp.float32)
    new_first = beta_one * first_moment + (1.0 - beta_one) * grad_full
    new_second = beta_two * second_moment + (1.0 - beta_two) * grad_full * grad_full
    update = new_first / correct_one / (jnp.sqrt(new_second / correct_two) + epsilon)
    return master * (1.0 - learn_rate * decay_rate) - learn_rate * update

def one_step(served, features, chosen, weights_raw):
    groups = N_DP * N_EXPERT
    routes = TOK_DEV * TOPK
    flat = chosen.reshape(groups, routes)
    onehot = (flat[:, :, None] == jnp.arange(EXPERTS, dtype=jnp.int32)[None, None, :]).astype(jnp.int32)
    position = lax.optimization_barrier(jnp.sum((jnp.cumsum(onehot, axis=1) - 1) * onehot, axis=2)).astype(jnp.int32)
    group_index = jnp.broadcast_to(jnp.arange(groups, dtype=jnp.int32)[:, None], (groups, routes))
    token_index = group_index * TOK_DEV + jnp.arange(routes, dtype=jnp.int32)[None, :] // TOPK
    table = jnp.full((EXPERTS, groups, CAP), -1, dtype=jnp.int32)
    table = table.at[flat, group_index, position].set(token_index)

    def per_expert(expert):
        rows = jnp.maximum(table[expert].reshape(-1), 0)
        picked = features[rows]
        product = jnp.dot(picked, served[expert], preferred_element_type=jnp.float32)
        return jax.nn.silu(product).astype(jnp.bfloat16)
    activations = lax.map(per_expert, jnp.arange(EXPERTS, dtype=jnp.int32))
    values = activations[flat, group_index * CAP + position]
    values = values.reshape(TOKENS, TOPK, F).astype(jnp.float32)
    shares = weights_raw / lax.optimization_barrier(jnp.sum(weights_raw, axis=1, keepdims=True))
    return lax.optimization_barrier(jnp.sum(shares[:, :, None] * values, axis=1)).astype(jnp.bfloat16)

def reference(master, first_moment, second_moment, gradient, tokens, expert_ids, router_scores):
    new_master = adam_update(master, first_moment, second_moment, gradient)
    served = new_master.astype(jnp.bfloat16)
    results = []
    for decode_step in range(STEPS):
        results.append(one_step(served, tokens[decode_step], expert_ids[decode_step], router_scores[decode_step]))
    return (new_master, jnp.stack(results))
```

```python
import jax
import jax.numpy as jnp
from jax import lax
from jax.experimental import pallas as pl
from jax.experimental.pallas import tpu as pltpu
from jax.sharding import Mesh, PartitionSpec as P

learn_rate = 0.01
decay_rate = 0.1
beta_one = 0.9
beta_two = 0.95
epsilon = 1e-08
correct_one = 1.0 - 0.9**4
correct_two = 1.0 - 0.95**4

TILE = 512


def adam_update(master, first_moment, second_moment, gradient):
    grad_full = gradient.astype(jnp.float32)
    new_first = beta_one * first_moment + (1.0 - beta_one) * grad_full
    new_second = beta_two * second_moment + (1.0 - beta_two) * grad_full * grad_full
    update = new_first / correct_one / (jnp.sqrt(new_second / correct_two) + epsilon)
    return master * (1.0 - learn_rate * decay_rate) - learn_rate * update


def expert_kernel(parts, which, first, last, *refs):
    tokens_ref, share_ref = refs[0], refs[1]
    weights = refs[2 : 2 + parts]
    total_ref = None if first else refs[2 + parts]
    out_ref = refs[-1]
    at = 0
    product = None
    for weight in weights:
        depth = weight.shape[0]
        piece = jnp.dot(
            tokens_ref[:, at : at + depth], weight[...], preferred_element_type=jnp.float32
        )
        product = piece if product is None else product + piece
        at += depth
    value = share_ref[:, which : which + 1] * (product * jax.nn.sigmoid(product))
    if not first:
        value = value + total_ref[...]
    if not last:
        out_ref[...] = value
        return
    groups, quarters, rows, width = out_ref.shape
    for group in range(groups):
        for quarter in range(quarters):
            out_ref[group, quarter] = value[
                group * rows : (group + 1) * rows, quarter * width : (quarter + 1) * width
            ].astype(out_ref.dtype)


def add_expert(tokens, shares, weights, which, total, out_shape, rows):
    count, depth = tokens.shape
    width = weights[0].shape[1]
    first, last = total is None, out_shape is not None
    in_specs = [
        pl.BlockSpec((TILE, depth), lambda i: (i, 0)),
        pl.BlockSpec((TILE, shares.shape[1]), lambda i: (i, 0)),
    ]
    in_specs += [pl.BlockSpec(w.shape, lambda i: (0, 0)) for w in weights]
    operands = [tokens, shares, *weights]
    if not first:
        in_specs.append(pl.BlockSpec((TILE, width), lambda i: (i, 0)))
        operands.append(total)
    if last:
        out = jax.ShapeDtypeStruct(out_shape, jnp.bfloat16)
        out_spec = pl.BlockSpec((TILE // rows,) + out_shape[1:], lambda i: (i, 0, 0, 0))
    else:
        out = jax.ShapeDtypeStruct((count, width), jnp.float32)
        out_spec = pl.BlockSpec((TILE, width), lambda i: (i, 0))

    def body(*refs):
        expert_kernel(len(weights), which, first, last, *refs)

    return pl.pallas_call(
        body,
        grid=(count // TILE,),
        in_specs=in_specs,
        out_specs=out_spec,
        out_shape=out,
        compiler_params=pltpu.CompilerParams(vmem_limit_bytes=40 * 2**20),
        cost_estimate=pl.CostEstimate(
            flops=2 * count * depth * width,
            bytes_accessed=2 * count * depth + 2 * depth * width + 8 * count * width,
            transcendentals=count * width,
        ),
    )(*operands)


def swap(value, offset):
    high, low = lax.axis_size("zh"), lax.axis_size("zl")
    pairs = []
    for z in range(offset, high * low + offset, low):
        a, b = [(at % low) * high + at // low % high for at in (z, z + 1)]
        pairs += [(a, b), (b, a)]
    return lax.ppermute(value, ("zl", "zh"), pairs)


def per_device(master, first_moment, second_moment, gradient, tokens, expert_ids, router_scores):
    steps, token_count, depth = tokens.shape
    quarters = lax.axis_size("x")
    cores = lax.axis_size("core")
    owners = lax.axis_size("zh")
    groups = cores * lax.axis_size("y")
    z_low, z_high = lax.axis_index("zl"), lax.axis_index("zh")
    y_at, x_at = lax.axis_index("y"), lax.axis_index("x")

    half = depth // 2
    flat = tokens.reshape(steps * token_count, depth)
    turned = jnp.where(
        z_low == 0, flat, jnp.concatenate([flat[:, half:], flat[:, :half]], axis=1)
    )
    all_tokens = lax.all_gather(turned, ("core", "y"), axis=0, tiled=True)

    ids = expert_ids.reshape(steps * token_count, -1)
    raw = router_scores.reshape(steps * token_count, -1)
    both = jnp.concatenate(
        [ids.astype(jnp.float32), raw / jnp.sum(raw, axis=1, keepdims=True)], axis=1
    )
    both = lax.all_gather(both, ("core", "y"), axis=0, tiled=True)
    choices = ids.shape[1]
    turn = jnp.where(z_low == 0, 1, -1)
    order = jnp.stack([z_high, z_high - turn, z_high + turn, z_high + 2])
    names = (quarters * (y_at * owners + jnp.mod(order, owners)) + x_at).astype(jnp.float32)
    shares = jnp.stack(
        [
            jnp.sum(jnp.where(both[:, :choices] == names[p], both[:, choices:], 0.0), axis=1)
            for p in range(4)
        ],
        axis=1,
    )

    new_master = adam_update(master, first_moment, second_moment, gradient)
    lowered = new_master.astype(jnp.bfloat16)
    experts, rows, width = lowered.shape
    strip = width // (quarters * cores)
    blocks = lowered.reshape(experts, rows, quarters, cores, strip)
    blocks = blocks.transpose(3, 0, 1, 2, 4).reshape(cores * experts, rows, quarters * strip)
    own = lax.all_to_all(blocks, ("core", "x"), split_axis=0, concat_axis=0, tiled=True)
    own = own.reshape(-1, quarters * strip)

    cut = own.shape[0] // 2
    a1, c1 = swap(own, 0), swap(own, 1)
    a2, c2 = swap(c1, 0), swap(a1, 1)
    a3, c3 = swap(c2, 0), swap(a2, 1)
    a4, c4 = swap(c3[:cut], 0), swap(a3[cut:], 1)

    total = add_expert(all_tokens, shares, [own, a1], 0, None, None, 0)
    total = add_expert(all_tokens, shares, [c2, c1], 1, total, None, 0)
    total = add_expert(all_tokens, shares, [a2, a3], 2, total, None, 0)
    out_shape = (groups, quarters, steps * token_count, strip)
    total = add_expert(
        all_tokens, shares, [a4, c4, c3], 3, total, out_shape, steps * token_count
    )
    total = total.reshape(groups * quarters, steps * token_count, strip)
    back = lax.all_to_all(total, ("core", "y", "x"), split_axis=0, concat_axis=0, tiled=True)
    back = back.reshape(cores, -1, steps, token_count, strip).astype(jnp.float32)
    mixed = jnp.sum(back, axis=1).astype(jnp.bfloat16)
    mixed = mixed.transpose(1, 2, 0, 3).reshape(steps, token_count, cores * strip)
    return (new_master, mixed)


def solution(mesh):
    grid = Mesh(mesh.devices.reshape(2, 2, 4, 4, 4), ("zl", "core", "y", "zh", "x"))
    owner, part, group = ("y", "zh"), ("zl", "core", "x"), ("zl", "core", "y", "zh")
    weights = P(owner, part, None)
    routed = P(None, group, None)
    return jax.shard_map(
        per_device,
        mesh=grid,
        in_specs=(weights,) * 4 + (routed,) * 3,
        out_specs=(weights, P(None, group, "x")),
        check_vma=False,
    )
```

```python
import jax
import jax.numpy as jnp
from jax import lax
from jax.experimental import pallas as pl
from jax.experimental.pallas import tpu as pltpu
from jax.sharding import Mesh, PartitionSpec as P

learn_rate = 0.01
decay_rate = 0.1
beta_one = 0.9
beta_two = 0.95
epsilon = 1e-08
correct_one = 1.0 - 0.9**4
correct_two = 1.0 - 0.95**4

CAP = 32
PARTS = 4
BIG = 40 * 2**20


def adam_update(master, first_moment, second_moment, gradient):
    grad_full = gradient.astype(jnp.float32)
    new_first = beta_one * first_moment + (1.0 - beta_one) * grad_full
    new_second = beta_two * second_moment + (1.0 - beta_two) * grad_full * grad_full
    update = new_first / correct_one / (jnp.sqrt(new_second / correct_two) + epsilon)
    return master * (1.0 - learn_rate * decay_rate) - learn_rate * update


def pick_kernel(where_ref, ids_ref, low_ref, high_ref, out_ref):
    steps, _, count = ids_ref.shape[2:]
    half = low_ref.shape[1]
    earlier = lax.broadcasted_iota(jnp.int32, (count, count), 0)
    later = lax.broadcasted_iota(jnp.int32, (count, count), 1)
    before = jnp.where(earlier < later, 1.0, 0.0).astype(jnp.bfloat16)
    slot = lax.broadcasted_iota(jnp.int32, (CAP, count), 0).astype(jnp.float32)
    for step in range(steps):
        ids = ids_ref[0, 0, step]
        masks = []
        for part in range(PARTS):
            hit = jnp.where(ids == where_ref[1 + part], 1.0, 0.0)
            masks.append(jnp.max(hit, axis=0, keepdims=True))
        mask = jnp.concatenate(masks * 2, axis=0)
        place = jnp.dot(
            mask.astype(jnp.bfloat16), before, preferred_element_type=jnp.float32
        )
        chosen = [
            jnp.where(slot == place[part : part + 1], mask[part : part + 1], 0.0)
            for part in range(PARTS)
        ]
        chosen = jnp.concatenate(chosen, axis=0).astype(jnp.bfloat16)
        rows = slice(step * count, (step + 1) * count)
        for at, ref in ((0, low_ref), (half, high_ref)):
            picked = jnp.dot(chosen, ref[rows, :], preferred_element_type=jnp.float32)
            picked = picked.astype(jnp.bfloat16)
            for part in range(PARTS):
                out_ref[part, step * CAP : (step + 1) * CAP, at : at + half] = picked[
                    part * CAP : (part + 1) * CAP
                ]


def pick_rows(where, all_ids, all_tokens, group_rows):
    ys, cores, steps, choices, count = all_ids.shape
    total, depth = all_tokens.shape
    half = depth // 2
    groups = total // group_rows
    return pl.pallas_call(
        pick_kernel,
        grid_spec=pltpu.PrefetchScalarGridSpec(
            num_scalar_prefetch=1,
            grid=(groups,),
            in_specs=[
                pl.BlockSpec(
                    (1, 1, steps, choices, count), lambda i, w: (i % ys, i // ys, 0, 0, 0)
                ),
                pl.BlockSpec((group_rows, half), lambda i, w: (i, w[0])),
                pl.BlockSpec((group_rows, half), lambda i, w: (i, 1 - w[0])),
            ],
            out_specs=pl.BlockSpec((PARTS, steps * CAP, depth), lambda i, w: (0, i, 0)),
        ),
        out_shape=jax.ShapeDtypeStruct((PARTS, groups * steps * CAP, depth), jnp.bfloat16),
        compiler_params=pltpu.CompilerParams(vmem_limit_bytes=BIG),
        cost_estimate=pl.CostEstimate(
            flops=8 * total * 128 * depth, bytes_accessed=4 * total * depth, transcendentals=0
        ),
    )(where, all_ids, all_tokens, all_tokens)


def expert_kernel(rows_ref, *refs):
    weights, out_ref = refs[:-1], refs[-1]
    at, product = 0, None
    for weight in weights:
        depth = weight.shape[0]
        piece = jnp.dot(
            rows_ref[0, :, at : at + depth], weight[...], preferred_element_type=jnp.float32
        )
        product = piece if product is None else product + piece
        at += depth
    value = (product * jax.nn.sigmoid(product)).astype(out_ref.dtype)
    groups, quarters, rows, width = out_ref.shape
    for group in range(groups):
        for quarter in range(quarters):
            out_ref[group, quarter] = value[
                group * rows : (group + 1) * rows, quarter * width : (quarter + 1) * width
            ]


def run_expert(picked, part, weights, groups, quarters):
    _, count, depth = picked.shape
    width = weights[0].shape[1]
    strip = width // quarters
    cuts = 2
    return pl.pallas_call(
        expert_kernel,
        grid=(cuts,),
        in_specs=[pl.BlockSpec((1, count, depth), lambda i: (part, 0, 0))]
        + [pl.BlockSpec((w.shape[0], width // cuts), lambda i: (0, i)) for w in weights],
        out_specs=pl.BlockSpec(
            (groups, quarters // cuts, count // groups, strip), lambda i: (0, i, 0, 0)
        ),
        out_shape=jax.ShapeDtypeStruct((groups, quarters, count // groups, strip), jnp.bfloat16),
        compiler_params=pltpu.CompilerParams(vmem_limit_bytes=BIG),
        cost_estimate=pl.CostEstimate(
            flops=2 * count * depth * width,
            bytes_accessed=2 * count * depth + 2 * depth * width + 2 * count * width,
            transcendentals=count * width,
        ),
    )(picked, *weights)


def place_kernel(order_ref, ids_ref, raw_ref, out_ref):
    count, choices = ids_ref.shape[1:]
    lanes = out_ref.shape[2]
    names = 128
    ids = ids_ref[0]
    raw = raw_ref[0]
    shares = raw / jnp.sum(raw, axis=1, keepdims=True)
    name = lax.broadcasted_iota(jnp.int32, (count, names), 1)
    mask = jnp.zeros((count, names), jnp.float32)
    weight = jnp.zeros((count, names), jnp.float32)
    for choice in range(choices):
        hit = ids[:, choice : choice + 1] == name
        mask = mask + jnp.where(hit, 1.0, 0.0)
        weight = weight + jnp.where(hit, shares[:, choice : choice + 1], 0.0)
    row = lax.broadcasted_iota(jnp.int32, (count, count), 0)
    column = lax.broadcasted_iota(jnp.int32, (count, count), 1)
    before = jnp.where(column < row, 1.0, 0.0).astype(jnp.bfloat16)
    place = jnp.dot(before, mask.astype(jnp.bfloat16), preferred_element_type=jnp.float32)
    place = jnp.where(mask > 0.0, place, 255.0).astype(jnp.bfloat16)
    high = weight.astype(jnp.bfloat16)
    low = (weight - high.astype(jnp.float32)).astype(jnp.bfloat16)
    stacked = jnp.concatenate([place, high, low], axis=0)
    span = lanes // PARTS
    for part in range(PARTS):
        lane = lax.broadcasted_iota(jnp.int32, (names, span), 1)
        device = lane // CAP
        expert = (device // 4 * 4 + order_ref[part]) * 4 + device % 4
        spread = jnp.where(
            lax.broadcasted_iota(jnp.int32, (names, span), 0) == expert, 1.0, 0.0
        ).astype(jnp.bfloat16)
        wide = jnp.dot(stacked, spread, preferred_element_type=jnp.float32)
        slot = (lax.broadcasted_iota(jnp.int32, (count, span), 1) % CAP).astype(jnp.float32)
        here = wide[:count] == slot
        at = slice(part * span, (part + 1) * span)
        out_ref[0, :count, at] = jnp.where(here, wide[count : 2 * count], 0.0).astype(jnp.bfloat16)
        out_ref[0, count:, at] = jnp.where(here, wide[2 * count :], 0.0).astype(jnp.bfloat16)


def place_rows(order, ids, raw, lanes):
    steps, count, choices = ids.shape
    return pl.pallas_call(
        place_kernel,
        grid_spec=pltpu.PrefetchScalarGridSpec(
            num_scalar_prefetch=1,
            grid=(steps,),
            in_specs=[pl.BlockSpec((1, count, choices), lambda i, w: (i, 0, 0))] * 2,
            out_specs=pl.BlockSpec((1, 2 * count, lanes), lambda i, w: (i, 0, 0)),
        ),
        out_shape=jax.ShapeDtypeStruct((steps, 2 * count, lanes), jnp.bfloat16),
        compiler_params=pltpu.CompilerParams(vmem_limit_bytes=BIG),
        cost_estimate=pl.CostEstimate(
            flops=2 * steps * 3 * count * 128 * lanes,
            bytes_accessed=4 * steps * count * lanes,
            transcendentals=0,
        ),
    )(order, ids, raw)


def mix_kernel(place_ref, *refs):
    returned, out_ref = refs[:-1], refs[-1]
    steps, count, width = out_ref.shape
    for step in range(steps):
        total = None
        for part, ref in enumerate(returned):
            cores, devices, _, slots, strip = ref.shape
            span = devices * slots
            rows = jnp.concatenate(
                [ref[core, :, step].reshape(span, strip) for core in range(cores)], axis=1
            )
            piece = jnp.dot(
                place_ref[step, :, part * span : (part + 1) * span],
                rows,
                preferred_element_type=jnp.float32,
            )
            total = piece if total is None else total + piece
        out_ref[step] = (total[:count] + total[count:]).astype(out_ref.dtype)


def mix_rows(placed, returned, count, width):
    steps = placed.shape[0]
    return pl.pallas_call(
        mix_kernel,
        in_specs=[pl.BlockSpec(memory_space=pltpu.VMEM)] * (1 + len(returned)),
        out_specs=pl.BlockSpec(memory_space=pltpu.VMEM),
        out_shape=jax.ShapeDtypeStruct((steps, count, width), jnp.bfloat16),
        compiler_params=pltpu.CompilerParams(vmem_limit_bytes=BIG),
        cost_estimate=pl.CostEstimate(
            flops=4 * placed.size * width // 2, bytes_accessed=2 * placed.size, transcendentals=0
        ),
    )(placed, *returned)


def swap(value, offset):
    high, low = lax.axis_size("zh"), lax.axis_size("zl")
    pairs = []
    for z in range(offset, high * low + offset, low):
        a, b = [(at % low) * high + at // low % high for at in (z, z + 1)]
        pairs += [(a, b), (b, a)]
    return lax.ppermute(value, ("zl", "zh"), pairs)


def gather_ids(expert_ids):
    own = expert_ids.transpose(0, 2, 1)
    other = lax.ppermute(own, "core", [(0, 1), (1, 0)])
    first = lax.axis_index("core") == 0
    pair = jnp.stack([jnp.where(first, own, other), jnp.where(first, other, own)])
    size = lax.axis_size("y")
    ring = [pair]
    for away in range(1, size):
        ring.append(lax.ppermute(pair, "y", [((at + away) % size, at) for at in range(size)]))
    ring = jnp.stack(ring + ring)
    return lax.dynamic_slice_in_dim(ring, size - lax.axis_index("y"), size, axis=0)


def per_device(master, first_moment, second_moment, gradient, tokens, expert_ids, router_scores):
    steps, token_count, depth = tokens.shape
    quarters = lax.axis_size("x")
    cores = lax.axis_size("core")
    owners = lax.axis_size("zh")
    ys = lax.axis_size("y")
    groups = cores * ys
    z_low, z_high = lax.axis_index("zl"), lax.axis_index("zh")
    y_at, x_at = lax.axis_index("y"), lax.axis_index("x")

    all_tokens = lax.all_gather(
        tokens.reshape(steps * token_count, depth), ("core", "y"), axis=0, tiled=True
    )
    all_ids = gather_ids(expert_ids)

    turn = jnp.where(z_low == 0, 1, -1)
    order = jnp.mod(jnp.stack([z_high, z_high - turn, z_high + turn, z_high + 2]), owners)
    names = quarters * (y_at * owners + order) + x_at
    where = jnp.concatenate([z_low[None], names]).astype(jnp.int32)

    new_master = adam_update(master, first_moment, second_moment, gradient)
    lowered = new_master.astype(jnp.bfloat16)
    experts, rows, width = lowered.shape
    strip = width // (quarters * cores)
    blocks = lowered.reshape(experts, rows, quarters, cores, strip)
    blocks = blocks.transpose(3, 0, 1, 2, 4).reshape(cores * experts, rows, quarters * strip)
    blocks, all_ids = lax.optimization_barrier((blocks, all_ids))
    own = lax.all_to_all(blocks, ("core", "x"), split_axis=0, concat_axis=0, tiled=True)
    own = own.reshape(-1, quarters * strip)

    def expert(part, weights):
        acted = run_expert(picked, part, weights, groups, quarters)
        acted = acted.reshape(groups * quarters, steps * CAP, strip)
        back = lax.all_to_all(acted, ("core", "y", "x"), split_axis=0, concat_axis=0, tiled=True)
        return back.reshape(cores, ys * quarters, steps, CAP, strip)

    hold = lax.optimization_barrier
    a1, c1 = swap(own, 0), swap(own, 1)
    placed = place_rows(
        order.astype(jnp.int32), expert_ids, router_scores, PARTS * quarters * ys * CAP
    )
    a1, c1, placed = hold((a1, c1, placed))
    a2, c2 = swap(c1, 0), swap(a1, 1)
    picked = pick_rows(where, all_ids, all_tokens, steps * token_count)
    a2, c2, picked = hold((a2, c2, picked))
    a3, c3 = swap(c2, 0), swap(a2, 1)
    back1, back2 = expert(0, [own, a1]), expert(1, [c2, c1])
    a3, c3, back1, back2 = hold((a3, c3, back1, back2))
    cut = own.shape[0] // 2
    a4, c4 = swap(c3[:cut], 0), swap(a3[cut:], 1)
    back3 = expert(2, [a2, a3])
    a4, c4, back3 = hold((a4, c4, back3))
    returned = [back1, back2, back3, expert(3, [a4, c4, c3])]
    mixed = mix_rows(placed, returned, token_count, cores * strip)
    return (new_master, mixed)


def solution(mesh):
    grid = Mesh(mesh.devices.reshape(2, 2, 4, 4, 4), ("zl", "core", "y", "zh", "x"))
    owner, part, group = ("y", "zh"), ("zl", "core", "x"), ("zl", "core", "y", "zh")
    weights = P(owner, part, None)
    routed = P(None, group, None)
    return jax.shard_map(
        per_device,
        mesh=grid,
        in_specs=(weights,) * 4 + (routed,) * 3,
        out_specs=(weights, P(None, group, "x")),
        check_vma=False,
    )
```

```python
import functools

import jax
import jax.numpy as jnp
from jax import lax
from jax.experimental import pallas as pl
from jax.experimental.pallas import tpu as pltpu
from jax.sharding import Mesh, PartitionSpec as P

learn_rate = 0.01
decay_rate = 0.1
beta_one = 0.9
beta_two = 0.95
epsilon = 1e-08
correct_one = 1.0 - 0.9**4
correct_two = 1.0 - 0.95**4

CAP = 32
PARTS = 4
CHUNKS = 2
STRIP = 128
ROOM = 20 * 2**20


def adam_kernel(master_ref, first_ref, second_ref, gradient_ref, new_ref, *chunk_refs):
    grad_full = gradient_ref[0].astype(jnp.float32)
    new_first = beta_one * first_ref[0] + (1.0 - beta_one) * grad_full
    new_second = beta_two * second_ref[0] + (1.0 - beta_two) * grad_full * grad_full
    update = new_first / correct_one / (jnp.sqrt(new_second / correct_two) + epsilon)
    updated = master_ref[0] * (1.0 - learn_rate * decay_rate) - learn_rate * update
    new_ref[0] = updated
    lowered = updated.astype(jnp.bfloat16)
    cores, _, _, part = chunk_refs[0].shape
    at = 0
    for ref in chunk_refs:
        for start in range(0, part, STRIP):
            for core in range(cores):
                ref[core, 0, :, start : start + STRIP] = lowered[:, at : at + STRIP]
                at += STRIP


def adam(master, first_moment, second_moment, gradient, cores):
    experts, rows, width = master.shape
    part = width // (cores * CHUNKS)
    whole = pl.BlockSpec((1, rows, width), lambda i: (i, 0, 0))
    block = pl.BlockSpec((cores, 1, rows, part), lambda i: (0, i, 0, 0))
    chunk = jax.ShapeDtypeStruct((cores, experts, rows, part), jnp.bfloat16)
    return pl.pallas_call(
        adam_kernel,
        grid=(experts,),
        in_specs=[whole] * 4,
        out_specs=[whole] + [block] * CHUNKS,
        out_shape=[jax.ShapeDtypeStruct(master.shape, jnp.float32)] + [chunk] * CHUNKS,
        compiler_params=pltpu.CompilerParams(vmem_limit_bytes=ROOM),
        cost_estimate=pl.CostEstimate(
            flops=16 * master.size, bytes_accessed=20 * master.size, transcendentals=master.size
        ),
    )(master, first_moment, second_moment, gradient)


def pick_kernel(where_ref, ids_ref, low_ref, high_ref, out_ref):
    steps, _, count = ids_ref.shape[2:]
    half = low_ref.shape[1]
    earlier = lax.broadcasted_iota(jnp.int32, (count, count), 0)
    later = lax.broadcasted_iota(jnp.int32, (count, count), 1)
    before = jnp.where(earlier < later, 1.0, 0.0).astype(jnp.bfloat16)
    slot = lax.broadcasted_iota(jnp.int32, (CAP, count), 0).astype(jnp.float32)
    for step in range(steps):
        ids = ids_ref[0, 0, step]
        masks = []
        for part in range(PARTS):
            hit = jnp.where(ids == where_ref[3 + part], 1.0, 0.0)
            masks.append(jnp.max(hit, axis=0, keepdims=True))
        mask = jnp.concatenate(masks * 2, axis=0)
        place = jnp.dot(
            mask.astype(jnp.bfloat16), before, preferred_element_type=jnp.float32
        )
        chosen = [
            jnp.where(slot == place[part : part + 1], mask[part : part + 1], 0.0)
            for part in range(PARTS)
        ]
        chosen = jnp.concatenate(chosen, axis=0).astype(jnp.bfloat16)
        rows = slice(step * count, (step + 1) * count)
        for at, ref in ((0, low_ref), (half, high_ref)):
            picked = jnp.dot(chosen, ref[rows, :], preferred_element_type=jnp.float32)
            picked = picked.astype(jnp.bfloat16)
            for part in range(PARTS):
                out_ref[part, step * CAP : (step + 1) * CAP, at : at + half] = picked[
                    part * CAP : (part + 1) * CAP
                ]


def pick_rows(where, all_ids, all_tokens, group_rows):
    _, ys, steps, choices, count = all_ids.shape
    total, depth = all_tokens.shape
    half = depth // 2
    groups = total // group_rows
    return pl.pallas_call(
        pick_kernel,
        grid_spec=pltpu.PrefetchScalarGridSpec(
            num_scalar_prefetch=1,
            grid=(groups,),
            in_specs=[
                pl.BlockSpec(
                    (1, 1, steps, choices, count),
                    lambda i, w: ((i // ys + w[1]) % 2, (i % ys + ys - w[2]) % ys, 0, 0, 0),
                ),
                pl.BlockSpec((group_rows, half), lambda i, w: (i, w[0])),
                pl.BlockSpec((group_rows, half), lambda i, w: (i, 1 - w[0])),
            ],
            out_specs=pl.BlockSpec((PARTS, steps * CAP, depth), lambda i, w: (0, i, 0)),
        ),
        out_shape=jax.ShapeDtypeStruct((PARTS, groups * steps * CAP, depth), jnp.bfloat16),
        compiler_params=pltpu.CompilerParams(vmem_limit_bytes=ROOM),
        cost_estimate=pl.CostEstimate(
            flops=8 * total * 128 * depth, bytes_accessed=4 * total * depth, transcendentals=0
        ),
    )(where, all_ids, all_tokens, all_tokens)


def halves(picked_ref, part, even, odd):
    half = picked_ref.shape[2] // 2
    total = None
    for at, weight in ((0, even), (half, odd)):
        if weight is not None:
            rows = picked_ref[part, :, at : at + half]
            piece = jnp.dot(rows, weight[...], preferred_element_type=jnp.float32)
            total = piece if total is None else total + piece
    return total


def act(out_ref, slot, chunk, product):
    value = (product * jax.nn.sigmoid(product)).astype(out_ref.dtype)
    groups, _, _, rows, strip = out_ref.shape
    wide = value.shape[1] // strip
    for group in range(groups):
        for column in range(wide):
            out_ref[group, chunk * wide + column, slot] = value[
                group * rows : (group + 1) * rows, column * strip : (column + 1) * strip
            ]


def early_kernel(picked_ref, own_a, own_b, a1_a, a1_b, c2_a, c2_b, c1_a, c1_b, out_ref):
    for chunk, (even, odd) in enumerate(((own_a, a1_a), (own_b, a1_b))):
        act(out_ref, 0, chunk, halves(picked_ref, 0, even, odd))
    for chunk, (even, odd) in enumerate(((c2_a, c1_a), (c2_b, c1_b))):
        act(out_ref, 1, chunk, halves(picked_ref, 1, even, odd))


def later_kernel(picked_ref, a2_a, a2_b, a3_a, a3_b, c3_a, c3_b, out_ref, start_ref):
    for chunk, (even, odd) in enumerate(((a2_a, a3_a), (a2_b, a3_b))):
        act(out_ref, 0, chunk, halves(picked_ref, 2, even, odd))
    for chunk, odd in enumerate((c3_a, c3_b)):
        start_ref[chunk] = halves(picked_ref, 3, None, odd)


def last_kernel(picked_ref, z4_a, z4_b, acted_ref, start_ref, out_ref):
    out_ref[:, :, :1] = acted_ref[...]
    for chunk, even in enumerate((z4_a, z4_b)):
        act(out_ref, 1, chunk, start_ref[chunk] + halves(picked_ref, 3, even, None))


def run(body, operands, out_shape, flops):
    spec = pl.BlockSpec(memory_space=pltpu.VMEM)
    return pl.pallas_call(
        body,
        in_specs=[spec] * len(operands),
        out_specs=jax.tree.map(lambda _: spec, out_shape),
        out_shape=out_shape,
        compiler_params=pltpu.CompilerParams(vmem_limit_bytes=ROOM),
        cost_estimate=pl.CostEstimate(
            flops=flops,
            bytes_accessed=sum(2 * x.size for x in operands),
            transcendentals=0,
        ),
    )(*operands)


def place_kernel(order_ref, ids_ref, raw_ref, out_ref):
    count, choices = ids_ref.shape[1:]
    lanes = out_ref.shape[2]
    names = 128
    ids = ids_ref[0]
    raw = raw_ref[0]
    shares = raw / jnp.sum(raw, axis=1, keepdims=True)
    name = lax.broadcasted_iota(jnp.int32, (count, names), 1)
    mask = jnp.zeros((count, names), jnp.float32)
    weight = jnp.zeros((count, names), jnp.float32)
    for choice in range(choices):
        hit = ids[:, choice : choice + 1] == name
        mask = mask + jnp.where(hit, 1.0, 0.0)
        weight = weight + jnp.where(hit, shares[:, choice : choice + 1], 0.0)
    row = lax.broadcasted_iota(jnp.int32, (count, count), 0)
    column = lax.broadcasted_iota(jnp.int32, (count, count), 1)
    before = jnp.where(column < row, 1.0, 0.0).astype(jnp.bfloat16)
    place = jnp.dot(before, mask.astype(jnp.bfloat16), preferred_element_type=jnp.float32)
    place = jnp.where(mask > 0.0, place, 255.0).astype(jnp.bfloat16)
    high = weight.astype(jnp.bfloat16)
    low = (weight - high.astype(jnp.float32)).astype(jnp.bfloat16)
    stacked = jnp.concatenate([place, high, low], axis=0)
    span = lanes // PARTS
    for part in range(PARTS):
        lane = lax.broadcasted_iota(jnp.int32, (names, span), 1)
        device = lane // CAP
        expert = (device // 4 * 4 + order_ref[part]) * 4 + device % 4
        spread = jnp.where(
            lax.broadcasted_iota(jnp.int32, (names, span), 0) == expert, 1.0, 0.0
        ).astype(jnp.bfloat16)
        wide = jnp.dot(stacked, spread, preferred_element_type=jnp.float32)
        slot = (lax.broadcasted_iota(jnp.int32, (count, span), 1) % CAP).astype(jnp.float32)
        here = wide[:count] == slot
        at = slice(part * span, (part + 1) * span)
        out_ref[0, :count, at] = jnp.where(here, wide[count : 2 * count], 0.0).astype(jnp.bfloat16)
        out_ref[0, count:, at] = jnp.where(here, wide[2 * count :], 0.0).astype(jnp.bfloat16)


def place_rows(order, ids, raw, lanes):
    steps, count, choices = ids.shape
    return pl.pallas_call(
        place_kernel,
        grid_spec=pltpu.PrefetchScalarGridSpec(
            num_scalar_prefetch=1,
            grid=(steps,),
            in_specs=[pl.BlockSpec((1, count, choices), lambda i, w: (i, 0, 0))] * 2,
            out_specs=pl.BlockSpec((1, 2 * count, lanes), lambda i, w: (i, 0, 0)),
        ),
        out_shape=jax.ShapeDtypeStruct((steps, 2 * count, lanes), jnp.bfloat16),
        compiler_params=pltpu.CompilerParams(vmem_limit_bytes=ROOM),
        cost_estimate=pl.CostEstimate(
            flops=2 * steps * 3 * count * 128 * lanes,
            bytes_accessed=4 * steps * count * lanes,
            transcendentals=0,
        ),
    )(order, ids, raw)


def mix_kernel(first, final, place_ref, returned_ref, *refs):
    out_ref = refs[-1]
    steps, count, _ = out_ref.shape
    cores, devices, slots, _, rows, strip = returned_ref.shape
    span = devices * rows
    for step in range(steps):
        total = None
        for slot in range(slots):
            part = first + slot
            arrived = jnp.concatenate(
                [returned_ref[c, :, slot, step].reshape(span, strip) for c in range(cores)], axis=1
            )
            piece = jnp.dot(
                place_ref[step, :, part * span : (part + 1) * span],
                arrived,
                preferred_element_type=jnp.float32,
            )
            total = piece if total is None else total + piece
        total = total[:count] + total[count:]
        if final:
            total = total + refs[0][step]
        out_ref[step] = total.astype(out_ref.dtype)


def swap(value, offset):
    high, low = lax.axis_size("zh"), lax.axis_size("zl")
    pairs = []
    for z in range(offset, high * low + offset, low):
        a, b = [(at % low) * high + at // low % high for at in (z, z + 1)]
        pairs += [(a, b), (b, a)]
    return lax.ppermute(value, ("zl", "zh"), pairs)


def along_y(expert_ids):
    own = expert_ids.transpose(0, 2, 1)
    size = lax.axis_size("y")
    ring = [own]
    for away in range(1, size):
        ring.append(lax.ppermute(own, "y", [((at + away) % size, at) for at in range(size)]))
    return jnp.stack(ring)


def per_device(master, first_moment, second_moment, gradient, tokens, expert_ids, router_scores):
    steps, token_count, depth = tokens.shape
    quarters = lax.axis_size("x")
    cores = lax.axis_size("core")
    owners = lax.axis_size("zh")
    ys = lax.axis_size("y")
    groups = cores * ys
    z_low, z_high = lax.axis_index("zl"), lax.axis_index("zh")
    y_at, x_at = lax.axis_index("y"), lax.axis_index("x")

    all_tokens = lax.all_gather(
        tokens.reshape(steps * token_count, depth), ("core", "y"), axis=0, tiled=True
    )
    near_ids = along_y(expert_ids)

    turn = jnp.where(z_low == 0, 1, -1)
    order = jnp.mod(jnp.stack([z_high, z_high - turn, z_high + turn, z_high + 2]), owners)
    names = quarters * (y_at * owners + order) + x_at
    here = jnp.stack([z_low, lax.axis_index("core"), y_at])
    where = jnp.concatenate([here, names]).astype(jnp.int32)

    new_master, *chunks = adam(master, first_moment, second_moment, gradient, cores)
    rows, width = master.shape[1:]
    part = width // (cores * CHUNKS)
    strip = width // (quarters * cores)
    chunks = [chunk.reshape(-1, rows, part) for chunk in chunks]

    def share_out(chunk):
        moved = lax.all_to_all(chunk, ("core", "x"), split_axis=0, concat_axis=0, tiled=True)
        return moved.reshape(-1, part)

    hold = lax.optimization_barrier
    first_chunk, near_ids = hold((chunks[0], near_ids))
    own_a = share_out(first_chunk)
    far_ids = lax.ppermute(near_ids, "core", [(0, 1), (1, 0)])
    own_a, all_ids = hold((own_a, jnp.stack([near_ids, far_ids])))
    a1_a, c1_a = swap(own_a, 0), swap(own_a, 1)
    own_b = share_out(chunks[1])
    a1_b, c1_b = swap(own_b, 0), swap(own_b, 1)
    placed = place_rows(
        order.astype(jnp.int32), expert_ids, router_scores, PARTS * quarters * ys * CAP
    )
    a1_a, c1_a = hold((a1_a, c1_a))
    a2_a, c2_a = swap(c1_a, 0), swap(a1_a, 1)
    a1_b, c1_b, placed = hold((a1_b, c1_b, placed))
    a2_b, c2_b = swap(c1_b, 0), swap(a1_b, 1)
    picked = pick_rows(where, all_ids, all_tokens, steps * token_count)
    a2_a, c2_a = hold((a2_a, c2_a))
    a3_a, c3_a = swap(c2_a, 0), swap(a2_a, 1)
    a2_b, c2_b, picked = hold((a2_b, c2_b, picked))
    a3_b, c3_b = swap(c2_b, 0), swap(a2_b, 1)
    flops = 2 * picked.shape[1] * depth * width // cores
    acted = jax.ShapeDtypeStruct((groups, quarters, 2, steps * CAP, strip), jnp.bfloat16)
    single = jax.ShapeDtypeStruct((groups, quarters, 1, steps * CAP, strip), jnp.bfloat16)
    start = jax.ShapeDtypeStruct((CHUNKS, picked.shape[1], part), jnp.float32)

    def send_back(value):
        value = value.reshape(groups * quarters, 2 * steps * CAP, strip)
        back = lax.all_to_all(value, ("core", "y", "x"), split_axis=0, concat_axis=0, tiled=True)
        return back.reshape(cores, ys * quarters, 2, steps, CAP, strip)

    early = run(
        early_kernel, [picked, own_a, own_b, a1_a, a1_b, c2_a, c2_b, c1_a, c1_b], acted, 2 * flops
    )
    a3_a, c3_a = hold((a3_a, c3_a))
    z4_a = swap(c3_a, 0)
    a3_b, c3_b, early = hold((a3_b, c3_b, early))
    early = send_back(early)
    z4_b = swap(a3_b, 1)
    later, begun = run(
        later_kernel, [picked, a2_a, a2_b, a3_a, a3_b, c3_a, c3_b], [single, start], 3 * flops // 2
    )
    mixed_shape = (steps, token_count, cores * strip)
    half_mixed = run(
        functools.partial(mix_kernel, 0, False),
        [placed, early],
        jax.ShapeDtypeStruct(mixed_shape, jnp.float32),
        2 * placed.size * cores * strip // 2,
    )
    z4_a, z4_b, later, begun, half_mixed = hold((z4_a, z4_b, later, begun, half_mixed))
    final = send_back(run(last_kernel, [picked, z4_a, z4_b, later, begun], acted, flops // 2))
    mixed = run(
        functools.partial(mix_kernel, 2, True),
        [placed, final, half_mixed],
        jax.ShapeDtypeStruct(mixed_shape, jnp.bfloat16),
        2 * placed.size * cores * strip // 2,
    )
    return (new_master, mixed)


def solution(mesh):
    grid = Mesh(mesh.devices.reshape(2, 2, 4, 4, 4), ("zl", "core", "y", "zh", "x"))
    owner, part, group = ("y", "zh"), ("zl", "core", "x"), ("zl", "core", "y", "zh")
    weights = P(owner, part, None)
    routed = P(None, group, None)
    return jax.shard_map(
        per_device,
        mesh=grid,
        in_specs=(weights,) * 4 + (routed,) * 3,
        out_specs=(weights, P(None, group, "x")),
        check_vma=False,
    )
```

```python
import functools

import jax
import jax.numpy as jnp
from jax import lax
from jax.experimental import pallas as pl
from jax.experimental.pallas import tpu as pltpu
from jax.sharding import Mesh, PartitionSpec as P

learn_rate = 0.01
decay_rate = 0.1
beta_one = 0.9
beta_two = 0.95
epsilon = 1e-08
correct_one = 1.0 - 0.9**4
correct_two = 1.0 - 0.95**4

CAP = 32
PARTS = 4
CHUNKS = 2
STRIP = 128
ROOM = 12 * 2**20
WIDE = 56 * 2**20
SMALL = pl.CostEstimate(flops=1, bytes_accessed=1, transcendentals=0)


def adam_kernel(master_ref, first_ref, second_ref, gradient_ref, new_ref, *chunk_refs):
    grad_full = gradient_ref[0].astype(jnp.float32)
    new_first = beta_one * first_ref[0] + (1.0 - beta_one) * grad_full
    new_second = beta_two * second_ref[0] + (1.0 - beta_two) * grad_full * grad_full
    update = new_first / correct_one / (jnp.sqrt(new_second / correct_two) + epsilon)
    updated = master_ref[0] * (1.0 - learn_rate * decay_rate) - learn_rate * update
    new_ref[0] = updated
    lowered = updated.astype(jnp.bfloat16)
    cores, _, _, part = chunk_refs[0].shape
    at = 0
    for ref in chunk_refs:
        for start in range(0, part, STRIP):
            for core in range(cores):
                ref[core, 0, :, start : start + STRIP] = lowered[:, at : at + STRIP]
                at += STRIP


def adam(master, first_moment, second_moment, gradient, cores):
    experts, rows, width = master.shape
    part = width // (cores * CHUNKS)
    whole = pl.BlockSpec((1, rows, width), lambda i: (i, 0, 0))
    block = pl.BlockSpec((cores, 1, rows, part), lambda i: (0, i, 0, 0))
    chunk = jax.ShapeDtypeStruct((cores, experts, rows, part), jnp.bfloat16)
    return pl.pallas_call(
        adam_kernel,
        grid=(experts,),
        in_specs=[whole] * 4,
        out_specs=[whole] + [block] * CHUNKS,
        out_shape=[jax.ShapeDtypeStruct(master.shape, jnp.float32)] + [chunk] * CHUNKS,
        compiler_params=pltpu.CompilerParams(vmem_limit_bytes=WIDE),
        cost_estimate=pl.CostEstimate(
            flops=16 * master.size, bytes_accessed=20 * master.size, transcendentals=master.size
        ),
    )(master, first_moment, second_moment, gradient)


def pick_kernel(where_ref, ids_ref, *refs):
    sides, ys, _, _, count = ids_ref.shape
    token_refs, out_refs = refs[: sides * ys], refs[sides * ys :]
    parts = len(out_refs)
    earlier = lax.broadcasted_iota(jnp.int32, (count, count), 0)
    later = lax.broadcasted_iota(jnp.int32, (count, count), 1)
    before = jnp.where(earlier < later, 1.0, 0.0).astype(jnp.bfloat16)
    slot = lax.broadcasted_iota(jnp.int32, (CAP, count), 0).astype(jnp.float32)
    masks = []
    groups = [(side, away) for side in range(sides) for away in range(ys)]
    for side, away in groups:
        ids = ids_ref[side, away, 0]
        for part in range(parts):
            hit = jnp.where(ids == where_ref[1 + part], 1.0, 0.0)
            masks.append(jnp.max(hit, axis=0, keepdims=True))
    mask = jnp.concatenate(masks, axis=0)
    place = jnp.dot(mask.astype(jnp.bfloat16), before, preferred_element_type=jnp.float32)
    for at, (side, away) in enumerate(groups):
        lines = [slice(at * parts + part, at * parts + part + 1) for part in range(parts)]
        chosen = [jnp.where(slot == place[line], mask[line], 0.0) for line in lines]
        chosen = jnp.concatenate(chosen, axis=0).astype(jnp.bfloat16)
        picked = jnp.dot(chosen, token_refs[at][0], preferred_element_type=jnp.float32)
        picked = picked.astype(jnp.bfloat16)
        for part in range(parts):
            out_refs[part][side, away] = picked[part * CAP : (part + 1) * CAP]


def pick_rows(where, ids, tokens):
    sides, ys, steps, choices, count = ids.shape
    depth = tokens[0].shape[2]
    half = depth // 2
    out = jax.ShapeDtypeStruct((sides, ys, steps * CAP, depth), jnp.bfloat16)
    return pl.pallas_call(
        pick_kernel,
        grid_spec=pltpu.PrefetchScalarGridSpec(
            num_scalar_prefetch=1,
            grid=(steps, 2),
            in_specs=[pl.BlockSpec((sides, ys, 1, choices, count), lambda i, j, w: (0, 0, i, 0, 0))]
            + [pl.BlockSpec((1, count, half), lambda i, j, w: (i, 0, (j + w[0]) % 2))]
            * (sides * ys),
            out_specs=[pl.BlockSpec((sides, ys, CAP, half), lambda i, j, w: (0, 0, i, j))] * PARTS,
        ),
        out_shape=[out] * PARTS,
        compiler_params=pltpu.CompilerParams(vmem_limit_bytes=2 * ROOM),
        cost_estimate=SMALL,
    )(where, ids, *tokens)


def halves(rows_ref, even, odd):
    sides, ys, count, depth = rows_ref.shape
    half = depth // 2
    total = None
    for at, weight in ((0, even), (half, odd)):
        if weight is not None:
            rows = rows_ref[:, :, :, at : at + half].reshape(sides * ys * count, half)
            piece = jnp.dot(rows, weight[...], preferred_element_type=jnp.float32)
            total = piece if total is None else total + piece
    return total


def act(out_ref, places, slot, chunk, product):
    value = (product * jax.nn.sigmoid(product)).astype(out_ref.dtype)
    _, _, _, rows, strip = out_ref.shape
    wide = value.shape[1] // strip
    for away, place in enumerate(places):
        for column in range(wide):
            out_ref[place, chunk * wide + column, slot] = value[
                away * rows : (away + 1) * rows, column * strip : (column + 1) * strip
            ]


def around(at_ref, rows_ref):
    cores, ys = rows_ref.shape[:2]
    core, y = at_ref[0], at_ref[1]
    return [
        lax.rem(core + side, cores) * ys + lax.rem(y + away, ys)
        for side in range(cores)
        for away in range(ys)
    ]


def early_kernel(at_ref, rows_0, rows_1, own_a, own_b, a1_a, a1_b, c2_a, c2_b, c1_a, c1_b, out_ref):
    places = around(at_ref, rows_0)
    for chunk, (even, odd) in enumerate(((own_a, a1_a), (own_b, a1_b))):
        act(out_ref, places, 0, chunk, halves(rows_0, even, odd))
    for chunk, (even, odd) in enumerate(((c2_a, c1_a), (c2_b, c1_b))):
        act(out_ref, places, 1, chunk, halves(rows_1, even, odd))


def later_kernel(at_ref, rows_2, a2_a, a2_b, a3_a, a3_b, out_ref):
    places = around(at_ref, rows_2)
    for chunk, (even, odd) in enumerate(((a2_a, a3_a), (a2_b, a3_b))):
        act(out_ref, places, 0, chunk, halves(rows_2, even, odd))


def begin_kernel(rows_3, c3_a, c3_b, start_ref):
    for chunk, odd in enumerate((c3_a, c3_b)):
        start_ref[chunk] = halves(rows_3, None, odd)


def last_kernel(at_ref, rows_3, z4_a, z4_b, start_ref, out_ref):
    places = around(at_ref, rows_3)
    for chunk, even in enumerate((z4_a, z4_b)):
        act(out_ref, places, 0, chunk, start_ref[chunk] + halves(rows_3, even, None))


def run(body, operands, out_shape, scalars=None):
    spec = pl.BlockSpec(memory_space=pltpu.VMEM)
    in_specs = [spec] * len(operands)
    if scalars is not None:
        in_specs = [pl.BlockSpec(memory_space=pltpu.SMEM)] + in_specs
        operands = [scalars] + operands
    return pl.pallas_call(
        body,
        in_specs=in_specs,
        out_specs=spec,
        out_shape=out_shape,
        compiler_params=pltpu.CompilerParams(vmem_limit_bytes=ROOM),
        cost_estimate=SMALL,
    )(*operands)


def place_kernel(order_ref, ids_ref, raw_ref, out_ref):
    count, choices = ids_ref.shape[1:]
    lanes = out_ref.shape[2]
    names = 128
    ids = ids_ref[0]
    raw = raw_ref[0]
    shares = raw / jnp.sum(raw, axis=1, keepdims=True)
    name = lax.broadcasted_iota(jnp.int32, (count, names), 1)
    mask = jnp.zeros((count, names), jnp.float32)
    weight = jnp.zeros((count, names), jnp.float32)
    for choice in range(choices):
        hit = ids[:, choice : choice + 1] == name
        mask = mask + jnp.where(hit, 1.0, 0.0)
        weight = weight + jnp.where(hit, shares[:, choice : choice + 1], 0.0)
    row = lax.broadcasted_iota(jnp.int32, (count, count), 0)
    column = lax.broadcasted_iota(jnp.int32, (count, count), 1)
    before = jnp.where(column < row, 1.0, 0.0).astype(jnp.bfloat16)
    place = jnp.dot(before, mask.astype(jnp.bfloat16), preferred_element_type=jnp.float32)
    place = jnp.where(mask > 0.0, place, 255.0).astype(jnp.bfloat16)
    high = weight.astype(jnp.bfloat16)
    low = (weight - high.astype(jnp.float32)).astype(jnp.bfloat16)
    stacked = jnp.concatenate([place, high, low], axis=0)
    span = lanes // PARTS
    for part in range(PARTS):
        lane = lax.broadcasted_iota(jnp.int32, (names, span), 1)
        device = lane // CAP
        expert = (device // 4 * 4 + order_ref[part]) * 4 + device % 4
        spread = jnp.where(
            lax.broadcasted_iota(jnp.int32, (names, span), 0) == expert, 1.0, 0.0
        ).astype(jnp.bfloat16)
        wide = jnp.dot(stacked, spread, preferred_element_type=jnp.float32)
        slot = (lax.broadcasted_iota(jnp.int32, (count, span), 1) % CAP).astype(jnp.float32)
        here = wide[:count] == slot
        at = slice(part * span, (part + 1) * span)
        out_ref[0, :count, at] = jnp.where(here, wide[count : 2 * count], 0.0).astype(jnp.bfloat16)
        out_ref[0, count:, at] = jnp.where(here, wide[2 * count :], 0.0).astype(jnp.bfloat16)


def place_rows(order, ids, raw, lanes):
    steps, count, choices = ids.shape
    return pl.pallas_call(
        place_kernel,
        grid_spec=pltpu.PrefetchScalarGridSpec(
            num_scalar_prefetch=1,
            grid=(steps,),
            in_specs=[pl.BlockSpec((1, count, choices), lambda i, w: (i, 0, 0))] * 2,
            out_specs=pl.BlockSpec((1, 2 * count, lanes), lambda i, w: (i, 0, 0)),
        ),
        out_shape=jax.ShapeDtypeStruct((steps, 2 * count, lanes), jnp.bfloat16),
        compiler_params=pltpu.CompilerParams(vmem_limit_bytes=ROOM),
        cost_estimate=SMALL,
    )(order, ids, raw)


def mix_kernel(first, place_ref, *refs):
    out_ref = refs[-1]
    steps, count, _ = out_ref.shape
    for step in range(steps):
        part, total = first, None
        for ref in refs[:-1]:
            if len(ref.shape) == len(out_ref.shape):
                total = total + ref[step]
                continue
            cores, devices, slots, _, rows, strip = ref.shape
            span = devices * rows
            for slot in range(slots):
                arrived = jnp.concatenate(
                    [ref[core, :, slot, step].reshape(span, strip) for core in range(cores)], axis=1
                )
                piece = jnp.dot(
                    place_ref[step, :, part * span : (part + 1) * span],
                    arrived,
                    preferred_element_type=jnp.float32,
                )
                piece = piece[:count] + piece[count:]
                total = piece if total is None else total + piece
                part += 1
        out_ref[step] = total.astype(out_ref.dtype)


def swap(value, offset):
    high, low = lax.axis_size("zh"), lax.axis_size("zl")
    pairs = []
    for z in range(offset, high * low + offset, low):
        a, b = [(at % low) * high + at // low % high for at in (z, z + 1)]
        pairs += [(a, b), (b, a)]
    return lax.ppermute(value, ("zl", "zh"), pairs)


def from_y(value, away):
    size = lax.axis_size("y")
    return lax.ppermute(value, "y", [((at + away) % size, at) for at in range(size)])


def swap_cores(value):
    return lax.ppermute(value, "core", [(0, 1), (1, 0)])


def per_device(master, first_moment, second_moment, gradient, tokens, expert_ids, router_scores):
    steps, token_count, depth = tokens.shape
    quarters = lax.axis_size("x")
    cores = lax.axis_size("core")
    owners = lax.axis_size("zh")
    ys = lax.axis_size("y")
    groups = cores * ys
    z_low, z_high = lax.axis_index("zl"), lax.axis_index("zh")
    y_at, x_at = lax.axis_index("y"), lax.axis_index("x")

    turn = jnp.where(z_low == 0, 1, -1)
    order = jnp.mod(jnp.stack([z_high, z_high - turn, z_high + turn, z_high + 2]), owners)
    names = quarters * (y_at * owners + order) + x_at
    where = jnp.concatenate([z_low[None], names]).astype(jnp.int32)
    order = order.astype(jnp.int32)
    here = jnp.stack([lax.axis_index("core"), y_at]).astype(jnp.int32)

    next_up, next_down = from_y(tokens, 1), from_y(tokens, -1)
    ids = expert_ids.transpose(0, 2, 1)
    near_ids = jnp.stack([ids] + [from_y(ids, away) for away in range(1, ys)])
    new_master, *chunks = adam(master, first_moment, second_moment, gradient, cores)
    rows, width = master.shape[1:]
    part = width // (cores * CHUNKS)
    strip = width // (quarters * cores)
    chunks = [chunk.reshape(-1, rows, part) for chunk in chunks]

    def share_out(chunk):
        moved = lax.all_to_all(chunk, ("core", "x"), split_axis=0, concat_axis=0, tiled=True)
        return moved.reshape(-1, part)

    def send_back(value):
        slots = value.shape[2]
        value = value.reshape(groups * quarters, slots * steps * CAP, strip)
        back = lax.all_to_all(value, ("core", "y", "x"), split_axis=0, concat_axis=0, tiled=True)
        return back.reshape(cores, ys * quarters, slots, steps, CAP, strip)

    hold = lax.optimization_barrier
    first_chunk, near_ids = hold((chunks[0], near_ids))
    own_a = share_out(first_chunk)
    own_a, all_ids = hold((own_a, jnp.stack([near_ids, swap_cores(near_ids)])))
    a1_a, c1_a = swap(own_a, 0), swap(own_a, 1)
    own_b, next_up, next_down = hold((share_out(chunks[1]), next_up, next_down))
    near = [tokens, next_up, from_y(next_down, -1), next_down]
    a1_b, c1_b = swap(own_b, 0), swap(own_b, 1)
    placed = place_rows(order, expert_ids, router_scores, PARTS * quarters * ys * CAP)
    a1_a, c1_a = hold((a1_a, c1_a))
    a2_a, c2_a = swap(c1_a, 0), swap(a1_a, 1)
    a1_b, c1_b, placed = hold((a1_b, c1_b, placed))
    a2_b, c2_b = swap(c1_b, 0), swap(a1_b, 1)
    far = [swap_cores(value) for value in near]
    rows = pick_rows(where, all_ids, near + far)
    a2_a, c2_a = hold((a2_a, c2_a))
    a3_a, c3_a = swap(c2_a, 0), swap(a2_a, 1)
    a2_b, c2_b, *rows = hold((a2_b, c2_b, *rows))
    a3_b, c3_b = swap(c2_b, 0), swap(a2_b, 1)
    double = jax.ShapeDtypeStruct((groups, quarters, 2, steps * CAP, strip), jnp.bfloat16)
    single = jax.ShapeDtypeStruct((groups, quarters, 1, steps * CAP, strip), jnp.bfloat16)
    start = jax.ShapeDtypeStruct((CHUNKS, groups * steps * CAP, part), jnp.float32)
    early = [rows[0], rows[1], own_a, own_b, a1_a, a1_b, c2_a, c2_b, c1_a, c1_b]
    early = run(early_kernel, early, double, here)
    a3_a, c3_a = hold((a3_a, c3_a))
    z4_a = swap(c3_a, 0)
    a3_b, c3_b, early = hold((a3_b, c3_b, early))
    early = send_back(early)
    z4_b = swap(a3_b, 1)
    later = send_back(run(later_kernel, [rows[2], a2_a, a2_b, a3_a, a3_b], single, here))
    begun = run(begin_kernel, [rows[3], c3_a, c3_b], start)
    mixed_shape = (steps, token_count, cores * strip)
    half_mixed = jax.ShapeDtypeStruct(mixed_shape, jnp.float32)
    half_mixed = run(functools.partial(mix_kernel, 0), [placed, early], half_mixed)
    z4_a, z4_b, begun, half_mixed = hold((z4_a, z4_b, begun, half_mixed))
    final = send_back(run(last_kernel, [rows[3], z4_a, z4_b, begun], single, here))
    mixed = jax.ShapeDtypeStruct(mixed_shape, jnp.bfloat16)
    mixed = run(functools.partial(mix_kernel, 2), [placed, later, final, half_mixed], mixed)
    return (new_master, mixed)


def solution(mesh):
    grid = Mesh(mesh.devices.reshape(2, 2, 4, 4, 4), ("zl", "core", "y", "zh", "x"))
    owner, part, group = ("y", "zh"), ("zl", "core", "x"), ("zl", "core", "y", "zh")
    weights = P(owner, part, None)
    routed = P(None, group, None)
    return jax.shard_map(
        per_device,
        mesh=grid,
        in_specs=(weights,) * 4 + (routed,) * 3,
        out_specs=(weights, P(None, group, "x")),
        check_vma=False,
    )
```

```python
import functools

import jax
import jax.numpy as jnp
from jax import lax
from jax.experimental import pallas as pl
from jax.experimental.pallas import tpu as pltpu
from jax.sharding import Mesh, PartitionSpec as P

learn_rate = 0.01
decay_rate = 0.1
beta_one = 0.9
beta_two = 0.95
epsilon = 1e-08
correct_one = 1.0 - 0.9**4
correct_two = 1.0 - 0.95**4

CAP = 32
PARTS = 4
STRIP = 128
ROOM = 20 * 2**20
WIDE = 56 * 2**20
SMALL = pl.CostEstimate(flops=1, bytes_accessed=1, transcendentals=0)


def adam_kernel(master_ref, first_ref, second_ref, gradient_ref, new_ref, block_ref):
    grad_full = gradient_ref[0].astype(jnp.float32)
    new_first = beta_one * first_ref[0] + (1.0 - beta_one) * grad_full
    new_second = beta_two * second_ref[0] + (1.0 - beta_two) * grad_full * grad_full
    update = new_first / correct_one / (jnp.sqrt(new_second / correct_two) + epsilon)
    updated = master_ref[0] * (1.0 - learn_rate * decay_rate) - learn_rate * update
    new_ref[0] = updated
    lowered = updated.astype(jnp.bfloat16)
    cores, _, _, part = block_ref.shape
    at = 0
    for start in range(0, part, STRIP):
        for core in range(cores):
            block_ref[core, 0, :, start : start + STRIP] = lowered[:, at : at + STRIP]
            at += STRIP


def adam(master, first_moment, second_moment, gradient, cores):
    experts, rows, width = master.shape
    part = width // cores
    whole = pl.BlockSpec((1, rows, width), lambda i: (i, 0, 0))
    block = pl.BlockSpec((cores, 1, rows, part), lambda i: (0, i, 0, 0))
    chunk = jax.ShapeDtypeStruct((cores, experts, rows, part), jnp.bfloat16)
    return pl.pallas_call(
        adam_kernel,
        grid=(experts,),
        in_specs=[whole] * 4,
        out_specs=[whole, block],
        out_shape=[jax.ShapeDtypeStruct(master.shape, jnp.float32)] + [chunk],
        compiler_params=pltpu.CompilerParams(vmem_limit_bytes=WIDE),
        cost_estimate=pl.CostEstimate(
            flops=16 * master.size, bytes_accessed=20 * master.size, transcendentals=master.size
        ),
    )(master, first_moment, second_moment, gradient)


def pick_kernel(where_ref, ids_ref, tokens_ref, out_ref):
    count = ids_ref.shape[2]
    ys, parts = out_ref.shape[:2]
    earlier = lax.broadcasted_iota(jnp.int32, (count, count), 0)
    later = lax.broadcasted_iota(jnp.int32, (count, count), 1)
    before = jnp.where(earlier < later, 1.0, 0.0).astype(jnp.bfloat16)
    slot = lax.broadcasted_iota(jnp.int32, (CAP, count), 0).astype(jnp.float32)
    ids = ids_ref[0]
    masks = []
    for at in range(ys * parts):
        hit = jnp.where(ids == where_ref[1 + at], 1.0, 0.0)
        masks.append(jnp.max(hit, axis=0, keepdims=True))
    mask = jnp.concatenate(masks, axis=0)
    place = jnp.dot(mask.astype(jnp.bfloat16), before, preferred_element_type=jnp.float32)
    chosen = [
        jnp.where(slot == place[at : at + 1], mask[at : at + 1], 0.0) for at in range(ys * parts)
    ]
    chosen = jnp.concatenate(chosen, axis=0).astype(jnp.bfloat16)
    picked = jnp.dot(chosen, tokens_ref[0], preferred_element_type=jnp.float32)
    picked = picked.astype(jnp.bfloat16)
    for y in range(ys):
        for part in range(parts):
            at = (y * parts + part) * CAP
            out_ref[y, part] = picked[at : at + CAP]


def pick_rows(where, ids, tokens, ys):
    steps, choices, count = ids.shape
    depth = tokens.shape[2]
    half = depth // 2
    out = jax.ShapeDtypeStruct((ys, PARTS, steps * CAP, depth), jnp.bfloat16)
    return pl.pallas_call(
        pick_kernel,
        grid_spec=pltpu.PrefetchScalarGridSpec(
            num_scalar_prefetch=1,
            grid=(steps, 2),
            in_specs=[
                pl.BlockSpec((1, choices, count), lambda i, j, w: (i, 0, 0)),
                pl.BlockSpec((1, count, half), lambda i, j, w: (i, 0, (j + w[0]) % 2)),
            ],
            out_specs=pl.BlockSpec((ys, PARTS, CAP, half), lambda i, j, w: (0, 0, i, j)),
        ),
        out_shape=out,
        compiler_params=pltpu.CompilerParams(vmem_limit_bytes=ROOM),
        cost_estimate=SMALL,
    )(where, ids, tokens)


def multiply(rows_ref, weights, at=0):
    sides, ys, count, _ = rows_ref.shape
    total = None
    for weight in weights:
        depth = weight.shape[0]
        rows = rows_ref[:, :, :, at : at + depth].reshape(sides * ys * count, depth)
        piece = jnp.dot(rows, weight[...], preferred_element_type=jnp.float32)
        total = piece if total is None else total + piece
        at += depth
    return total


def fetch(near, far, part, held, sems, slot=0):
    copies = []
    for side, ref in enumerate((near, far)):
        copy = pltpu.make_async_copy(ref.at[:, part], held.at[slot, side], sems.at[slot, side])
        copy.start()
        copies.append(copy)
    return copies


def wait(copies):
    for copy in copies:
        copy.wait()


def act(out_ref, places, slot, product):
    value = (product * jax.nn.sigmoid(product)).astype(out_ref.dtype)
    _, _, _, rows, strip = out_ref.shape
    for away, place in enumerate(places):
        for column in range(value.shape[1] // strip):
            out_ref[place, column, slot] = value[
                away * rows : (away + 1) * rows, column * strip : (column + 1) * strip
            ]


def around(core_ref, ys):
    return [lax.rem(core_ref[0] + side, 2) * ys + y for side in range(2) for y in range(ys)]


def early_kernel(core_ref, near, far, *refs):
    weights, (out_ref, held, sems) = refs[:-3], refs[-3:]
    first, second = [fetch(near, far, part, held, sems, part) for part in range(2)]
    places = around(core_ref, near.shape[0])
    wait(first)
    act(out_ref, places, 0, multiply(held.at[0], weights[:4]))
    wait(second)
    act(out_ref, places, 1, multiply(held.at[1], weights[4:]))


def later_kernel(core_ref, near, far, *refs):
    weights, (out_ref, held, sems) = refs[:-3], refs[-3:]
    wait(fetch(near, far, 2, held, sems))
    act(out_ref, around(core_ref, near.shape[0]), 0, multiply(held.at[0], weights))


def begin_kernel(core_ref, near, far, c3_a, c3_b, start_ref, held, sems):
    wait(fetch(near, far, 3, held, sems))
    start_ref[...] = multiply(held.at[0], [c3_a, c3_b], near.shape[3] // 2)


def last_kernel(core_ref, near, far, z4_a, z4_b, start_ref, out_ref, held, sems):
    wait(fetch(near, far, 3, held, sems))
    product = start_ref[...] + multiply(held.at[0], [z4_a, z4_b])
    act(out_ref, around(core_ref, near.shape[0]), 0, product)


def run(body, operands, out_shape, rows=None, core=None, slots=1):
    spec = pl.BlockSpec(memory_space=pltpu.VMEM)
    in_specs = [spec] * len(operands)
    scratch = []
    if rows is not None:
        in_specs = [
            pl.BlockSpec(memory_space=pltpu.SMEM),
            pl.BlockSpec(memory_space=pl.ANY),
            pl.BlockSpec(memory_space=pl.ANY),
        ] + in_specs
        operands = [core, *rows, *operands]
        ys, _, count, depth = rows[0].shape
        scratch = [
            pltpu.VMEM((slots, 2, ys, count, depth), jnp.bfloat16),
            pltpu.SemaphoreType.DMA((slots, 2)),
        ]
    return pl.pallas_call(
        body,
        in_specs=in_specs,
        out_specs=spec,
        out_shape=out_shape,
        scratch_shapes=scratch,
        compiler_params=pltpu.CompilerParams(vmem_limit_bytes=ROOM),
        cost_estimate=SMALL,
    )(*operands)


def place_kernel(order_ref, ids_ref, raw_ref, out_ref):
    count, choices = ids_ref.shape[1:]
    lanes = out_ref.shape[2]
    names = 128
    ids = ids_ref[0]
    raw = raw_ref[0]
    shares = raw / jnp.sum(raw, axis=1, keepdims=True)
    name = lax.broadcasted_iota(jnp.int32, (count, names), 1)
    mask = jnp.zeros((count, names), jnp.float32)
    weight = jnp.zeros((count, names), jnp.float32)
    for choice in range(choices):
        hit = ids[:, choice : choice + 1] == name
        mask = mask + jnp.where(hit, 1.0, 0.0)
        weight = weight + jnp.where(hit, shares[:, choice : choice + 1], 0.0)
    row = lax.broadcasted_iota(jnp.int32, (count, count), 0)
    column = lax.broadcasted_iota(jnp.int32, (count, count), 1)
    before = jnp.where(column < row, 1.0, 0.0).astype(jnp.bfloat16)
    place = jnp.dot(before, mask.astype(jnp.bfloat16), preferred_element_type=jnp.float32)
    place = jnp.where(mask > 0.0, place, 255.0).astype(jnp.bfloat16)
    high = weight.astype(jnp.bfloat16)
    low = (weight - high.astype(jnp.float32)).astype(jnp.bfloat16)
    stacked = jnp.concatenate([place, high, low], axis=0)
    span = lanes // PARTS
    for part in range(PARTS):
        lane = lax.broadcasted_iota(jnp.int32, (names, span), 1)
        device = lane // CAP
        expert = (device // 4 * 4 + order_ref[part]) * 4 + device % 4
        spread = jnp.where(
            lax.broadcasted_iota(jnp.int32, (names, span), 0) == expert, 1.0, 0.0
        ).astype(jnp.bfloat16)
        wide = jnp.dot(stacked, spread, preferred_element_type=jnp.float32)
        slot = (lax.broadcasted_iota(jnp.int32, (count, span), 1) % CAP).astype(jnp.float32)
        here = wide[:count] == slot
        at = slice(part * span, (part + 1) * span)
        out_ref[0, :count, at] = jnp.where(here, wide[count : 2 * count], 0.0).astype(jnp.bfloat16)
        out_ref[0, count:, at] = jnp.where(here, wide[2 * count :], 0.0).astype(jnp.bfloat16)


def place_rows(order, ids, raw, lanes):
    steps, count, choices = ids.shape
    return pl.pallas_call(
        place_kernel,
        grid_spec=pltpu.PrefetchScalarGridSpec(
            num_scalar_prefetch=1,
            grid=(steps,),
            in_specs=[pl.BlockSpec((1, count, choices), lambda i, w: (i, 0, 0))] * 2,
            out_specs=pl.BlockSpec((1, 2 * count, lanes), lambda i, w: (i, 0, 0)),
        ),
        out_shape=jax.ShapeDtypeStruct((steps, 2 * count, lanes), jnp.bfloat16),
        compiler_params=pltpu.CompilerParams(vmem_limit_bytes=ROOM),
        cost_estimate=SMALL,
    )(order, ids, raw)


def mix_kernel(first, place_ref, *refs):
    out_ref = refs[-1]
    steps, count, _ = out_ref.shape
    for step in range(steps):
        part, total = first, None
        for ref in refs[:-1]:
            if len(ref.shape) == len(out_ref.shape):
                total = total + ref[step]
                continue
            cores, devices, slots, _, rows, strip = ref.shape
            span = devices * rows
            for slot in range(slots):
                arrived = jnp.concatenate(
                    [ref[core, :, slot, step].reshape(span, strip) for core in range(cores)], axis=1
                )
                piece = jnp.dot(
                    place_ref[step, :, part * span : (part + 1) * span],
                    arrived,
                    preferred_element_type=jnp.float32,
                )
                piece = piece[:count] + piece[count:]
                total = piece if total is None else total + piece
                part += 1
        out_ref[step] = total.astype(out_ref.dtype)


def swap(value, offset):
    high, low = lax.axis_size("zh"), lax.axis_size("zl")
    pairs = []
    for z in range(offset, high * low + offset, low):
        a, b = [(at % low) * high + at // low % high for at in (z, z + 1)]
        pairs += [(a, b), (b, a)]
    return lax.ppermute(value, ("zl", "zh"), pairs)


def swap_cores(value):
    return lax.ppermute(value, "core", [(0, 1), (1, 0)])


def per_device(master, first_moment, second_moment, gradient, tokens, expert_ids, router_scores):
    steps, token_count, depth = tokens.shape
    quarters = lax.axis_size("x")
    cores = lax.axis_size("core")
    owners = lax.axis_size("zh")
    ys = lax.axis_size("y")
    groups = cores * ys
    z_low, z_high = lax.axis_index("zl"), lax.axis_index("zh")
    x_at = lax.axis_index("x")

    turn = jnp.where(z_low == 0, 1, -1)
    order = jnp.mod(jnp.stack([z_high, z_high - turn, z_high + turn, z_high + 2]), owners)
    names = quarters * (jnp.arange(ys)[:, None] * owners + order[None, :]) + x_at
    where = jnp.concatenate([z_low[None], names.reshape(-1)]).astype(jnp.int32)
    order = order.astype(jnp.int32)
    core = lax.axis_index("core").reshape(1).astype(jnp.int32)

    new_master, blocks = adam(master, first_moment, second_moment, gradient, cores)
    rows, width = master.shape[1:]
    part = width // cores
    strip = width // (quarters * cores)

    hold = lax.optimization_barrier
    blocks, tokens = hold((blocks.reshape(-1, rows, part), tokens))
    own = lax.all_to_all(blocks, ("core", "x"), split_axis=0, concat_axis=0, tiled=True)
    picked = pick_rows(where, expert_ids.transpose(0, 2, 1), tokens, ys)
    own, picked = hold((own, picked))
    near = lax.all_to_all(picked, "y", split_axis=0, concat_axis=0, tiled=True)
    own = own.reshape(-1, part)
    cut = own.shape[0] // 2
    own_a, own_b = own[:cut], own[cut:]
    a1_a, c1_a = swap(own_a, 0), swap(own_a, 1)
    a1_b, c1_b = swap(own_b, 0), swap(own_b, 1)
    placed = place_rows(order, expert_ids, router_scores, PARTS * quarters * ys * CAP)
    a1_a, c1_a = hold((a1_a, c1_a))
    a2_a, c2_a = swap(c1_a, 0), swap(a1_a, 1)
    a1_b, c1_b, placed, used_1 = hold((a1_b, c1_b, placed, a1_a))
    a2_b, c2_b = swap(c1_b, 0), swap(a1_b, 1)
    a2_a, c2_a = hold((a2_a, c2_a))
    a3_a, c3_a = swap(c2_a, 0), swap(a2_a, 1)
    a2_b, c2_b, used_2, near = hold((a2_b, c2_b, a2_a, near))
    a3_b, c3_b = swap(c2_b, 0), swap(a2_b, 1)
    sides = (near, swap_cores(near))
    double = jax.ShapeDtypeStruct((groups, quarters, 2, steps * CAP, strip), jnp.bfloat16)
    single = jax.ShapeDtypeStruct((groups, quarters, 1, steps * CAP, strip), jnp.bfloat16)
    start = jax.ShapeDtypeStruct((groups * steps * CAP, part), jnp.float32)

    def send_back(value):
        slots = value.shape[2]
        value = value.reshape(groups * quarters, slots * steps * CAP, strip)
        back = lax.all_to_all(value, ("core", "y", "x"), split_axis=0, concat_axis=0, tiled=True)
        return back.reshape(cores, ys * quarters, slots, steps, CAP, strip)

    early = [own_a, own_b, used_1, a1_b, c2_a, c2_b, c1_a, c1_b]
    early = run(early_kernel, early, double, sides, core, 2)
    a3_a, c3_a = hold((a3_a, c3_a))
    z4_a = swap(c3_a, 0)
    a3_b, c3_b, early, used_3 = hold((a3_b, c3_b, early, a3_a))
    early = send_back(early)
    z4_b = swap(a3_b, 1)
    later = send_back(run(later_kernel, [used_2, a2_b, used_3, a3_b], single, sides, core))
    begun = run(begin_kernel, [c3_a, c3_b], start, sides, core)
    mixed_shape = (steps, token_count, cores * strip)
    half_mixed = jax.ShapeDtypeStruct(mixed_shape, jnp.float32)
    half_mixed = run(functools.partial(mix_kernel, 0), [placed, early], half_mixed)
    z4_a, z4_b, begun, half_mixed = hold((z4_a, z4_b, begun, half_mixed))
    final = send_back(run(last_kernel, [z4_a, z4_b, begun], single, sides, core))
    mixed = jax.ShapeDtypeStruct(mixed_shape, jnp.bfloat16)
    mixed = run(functools.partial(mix_kernel, 2), [placed, later, final, half_mixed], mixed)
    return (new_master, mixed)


def solution(mesh):
    grid = Mesh(mesh.devices.reshape(2, 2, 4, 4, 4), ("zl", "core", "y", "zh", "x"))
    owner, part, group = ("y", "zh"), ("zl", "core", "x"), ("zl", "core", "y", "zh")
    weights = P(owner, part, None)
    routed = P(None, group, None)
    return jax.shard_map(
        per_device,
        mesh=grid,
        in_specs=(weights,) * 4 + (routed,) * 3,
        out_specs=(weights, P(None, group, "x")),
        check_vma=False,
    )
```

```python
import functools

import jax
import jax.numpy as jnp
from jax import lax
from jax.experimental import pallas as pl
from jax.experimental.pallas import tpu as pltpu
from jax.sharding import Mesh, PartitionSpec as P

learn_rate = 0.01
decay_rate = 0.1
beta_one = 0.9
beta_two = 0.95
epsilon = 1e-08
correct_one = 1.0 - 0.9**4
correct_two = 1.0 - 0.95**4

CAP = 32
PARTS = 4
CHUNKS = 2
STRIP = 128
ROOM = 12 * 2**20
WIDE = 56 * 2**20
PICK = 44 * 2**20
SMALL = pl.CostEstimate(flops=1, bytes_accessed=1, transcendentals=0)


def adam_kernel(master_ref, first_ref, second_ref, gradient_ref, new_ref, *chunk_refs):
    grad_full = gradient_ref[0].astype(jnp.float32)
    new_first = beta_one * first_ref[0] + (1.0 - beta_one) * grad_full
    new_second = beta_two * second_ref[0] + (1.0 - beta_two) * grad_full * grad_full
    update = new_first / correct_one / (jnp.sqrt(new_second / correct_two) + epsilon)
    updated = master_ref[0] * (1.0 - learn_rate * decay_rate) - learn_rate * update
    new_ref[0] = updated
    lowered = updated.astype(jnp.bfloat16)
    cores, _, _, part = chunk_refs[0].shape
    at = 0
    for ref in chunk_refs:
        for start in range(0, part, STRIP):
            for core in range(cores):
                ref[core, 0, :, start : start + STRIP] = lowered[:, at : at + STRIP]
                at += STRIP


def adam(master, first_moment, second_moment, gradient, cores):
    experts, rows, width = master.shape
    part = width // (cores * CHUNKS)
    cut = rows // 2
    whole = pl.BlockSpec((1, cut, width), lambda i, j: (i, j, 0))
    block = pl.BlockSpec((cores, 1, cut, part), lambda i, j: (0, i, j, 0))
    chunk = jax.ShapeDtypeStruct((cores, experts, rows, part), jnp.bfloat16)
    return pl.pallas_call(
        adam_kernel,
        grid=(experts, 2),
        in_specs=[whole] * 4,
        out_specs=[whole] + [block] * CHUNKS,
        out_shape=[jax.ShapeDtypeStruct(master.shape, jnp.float32)] + [chunk] * CHUNKS,
        compiler_params=pltpu.CompilerParams(vmem_limit_bytes=WIDE),
        cost_estimate=pl.CostEstimate(
            flops=16 * master.size, bytes_accessed=20 * master.size, transcendentals=master.size
        ),
    )(master, first_moment, second_moment, gradient)


def pick_kernel(where_ref, ids_ref, low_ref, high_ref, *out_refs):
    steps, _, count = ids_ref.shape[2:]
    half = low_ref.shape[1]
    earlier = lax.broadcasted_iota(jnp.int32, (count, count), 0)
    later = lax.broadcasted_iota(jnp.int32, (count, count), 1)
    before = jnp.where(earlier < later, 1.0, 0.0).astype(jnp.bfloat16)
    slot = lax.broadcasted_iota(jnp.int32, (CAP, count), 0).astype(jnp.float32)
    for step in range(steps):
        ids = ids_ref[0, 0, step]
        masks = []
        for part in range(PARTS):
            hit = jnp.where(ids == where_ref[3 + part], 1.0, 0.0)
            masks.append(jnp.max(hit, axis=0, keepdims=True))
        mask = jnp.concatenate(masks * 2, axis=0)
        place = jnp.dot(
            mask.astype(jnp.bfloat16), before, preferred_element_type=jnp.float32
        )
        chosen = [
            jnp.where(slot == place[part : part + 1], mask[part : part + 1], 0.0)
            for part in range(PARTS)
        ]
        chosen = jnp.concatenate(chosen, axis=0).astype(jnp.bfloat16)
        rows = slice(step * count, (step + 1) * count)
        for at, ref in ((0, low_ref), (half, high_ref)):
            picked = jnp.dot(chosen, ref[rows, :], preferred_element_type=jnp.float32)
            picked = picked.astype(jnp.bfloat16)
            for part in range(PARTS):
                out_refs[part][step * CAP : (step + 1) * CAP, at : at + half] = picked[
                    part * CAP : (part + 1) * CAP
                ]


def pick_rows(where, all_ids, all_tokens, group_rows):
    _, ys, steps, choices, count = all_ids.shape
    total, depth = all_tokens.shape
    half = depth // 2
    groups = total // group_rows
    return pl.pallas_call(
        pick_kernel,
        grid_spec=pltpu.PrefetchScalarGridSpec(
            num_scalar_prefetch=1,
            grid=(groups,),
            in_specs=[
                pl.BlockSpec(
                    (1, 1, steps, choices, count),
                    lambda i, w: ((i // ys + w[1]) % 2, (i % ys + ys - w[2]) % ys, 0, 0, 0),
                ),
                pl.BlockSpec((group_rows, half), lambda i, w: (i, w[0])),
                pl.BlockSpec((group_rows, half), lambda i, w: (i, 1 - w[0])),
            ],
            out_specs=[pl.BlockSpec((steps * CAP, depth), lambda i, w: (i, 0))] * PARTS,
        ),
        out_shape=[jax.ShapeDtypeStruct((groups * steps * CAP, depth), jnp.bfloat16)] * PARTS,
        compiler_params=pltpu.CompilerParams(vmem_limit_bytes=PICK),
        cost_estimate=pl.CostEstimate(
            flops=8 * total * 128 * depth, bytes_accessed=4 * total * depth, transcendentals=0
        ),
    )(where, all_ids, all_tokens, all_tokens)


def halves(rows_ref, even, odd):
    half = rows_ref.shape[1] // 2
    total = None
    for at, weight in ((0, even), (half, odd)):
        if weight is not None:
            rows = rows_ref[:, at : at + half]
            piece = jnp.dot(rows, weight[...], preferred_element_type=jnp.float32)
            total = piece if total is None else total + piece
    return total


def act(out_ref, slot, chunk, product):
    value = (product * jax.nn.sigmoid(product)).astype(out_ref.dtype)
    groups, _, _, rows, strip = out_ref.shape
    wide = value.shape[1] // strip
    for group in range(groups):
        for column in range(wide):
            out_ref[group, chunk * wide + column, slot] = value[
                group * rows : (group + 1) * rows, column * strip : (column + 1) * strip
            ]


def early_kernel(rows_0, rows_1, own_a, own_b, a1_a, a1_b, c2_a, c2_b, c1_a, c1_b, out_ref):
    for chunk, (even, odd) in enumerate(((own_a, a1_a), (own_b, a1_b))):
        act(out_ref, 0, chunk, halves(rows_0, even, odd))
    for chunk, (even, odd) in enumerate(((c2_a, c1_a), (c2_b, c1_b))):
        act(out_ref, 1, chunk, halves(rows_1, even, odd))


def later_kernel(rows_2, a2_a, a2_b, a3_a, a3_b, out_ref):
    for chunk, (even, odd) in enumerate(((a2_a, a3_a), (a2_b, a3_b))):
        act(out_ref, 0, chunk, halves(rows_2, even, odd))


def begin_kernel(rows_3, c3_a, c3_b, start_ref):
    for chunk, odd in enumerate((c3_a, c3_b)):
        start_ref[chunk] = halves(rows_3, None, odd)


def last_kernel(rows_3, z4_a, z4_b, start_ref, acted_ref, out_ref):
    out_ref[:, :, :1] = acted_ref[...]
    for chunk, even in enumerate((z4_a, z4_b)):
        act(out_ref, 1, chunk, start_ref[chunk] + halves(rows_3, even, None))


def run(body, operands, out_shape):
    spec = pl.BlockSpec(memory_space=pltpu.VMEM)
    return pl.pallas_call(
        body,
        in_specs=[spec] * len(operands),
        out_specs=spec,
        out_shape=out_shape,
        compiler_params=pltpu.CompilerParams(vmem_limit_bytes=ROOM),
        cost_estimate=SMALL,
    )(*operands)


def place_kernel(order_ref, ids_ref, raw_ref, out_ref):
    count, choices = ids_ref.shape[1:]
    lanes = out_ref.shape[2]
    names = 128
    ids = ids_ref[0]
    raw = raw_ref[0]
    shares = raw / jnp.sum(raw, axis=1, keepdims=True)
    name = lax.broadcasted_iota(jnp.int32, (count, names), 1)
    mask = jnp.zeros((count, names), jnp.float32)
    weight = jnp.zeros((count, names), jnp.float32)
    for choice in range(choices):
        hit = ids[:, choice : choice + 1] == name
        mask = mask + jnp.where(hit, 1.0, 0.0)
        weight = weight + jnp.where(hit, shares[:, choice : choice + 1], 0.0)
    row = lax.broadcasted_iota(jnp.int32, (count, count), 0)
    column = lax.broadcasted_iota(jnp.int32, (count, count), 1)
    before = jnp.where(column < row, 1.0, 0.0).astype(jnp.bfloat16)
    place = jnp.dot(before, mask.astype(jnp.bfloat16), preferred_element_type=jnp.float32)
    place = jnp.where(mask > 0.0, place, 255.0).astype(jnp.bfloat16)
    high = weight.astype(jnp.bfloat16)
    low = (weight - high.astype(jnp.float32)).astype(jnp.bfloat16)
    stacked = jnp.concatenate([place, high, low], axis=0)
    span = lanes // PARTS
    for part in range(PARTS):
        lane = lax.broadcasted_iota(jnp.int32, (names, span), 1)
        device = lane // CAP
        expert = (device // 4 * 4 + order_ref[part]) * 4 + device % 4
        spread = jnp.where(
            lax.broadcasted_iota(jnp.int32, (names, span), 0) == expert, 1.0, 0.0
        ).astype(jnp.bfloat16)
        wide = jnp.dot(stacked, spread, preferred_element_type=jnp.float32)
        slot = (lax.broadcasted_iota(jnp.int32, (count, span), 1) % CAP).astype(jnp.float32)
        here = wide[:count] == slot
        at = slice(part * span, (part + 1) * span)
        out_ref[0, :count, at] = jnp.where(here, wide[count : 2 * count], 0.0).astype(jnp.bfloat16)
        out_ref[0, count:, at] = jnp.where(here, wide[2 * count :], 0.0).astype(jnp.bfloat16)


def place_rows(order, ids, raw, lanes):
    steps, count, choices = ids.shape
    return pl.pallas_call(
        place_kernel,
        grid_spec=pltpu.PrefetchScalarGridSpec(
            num_scalar_prefetch=1,
            grid=(steps,),
            in_specs=[pl.BlockSpec((1, count, choices), lambda i, w: (i, 0, 0))] * 2,
            out_specs=pl.BlockSpec((1, 2 * count, lanes), lambda i, w: (i, 0, 0)),
        ),
        out_shape=jax.ShapeDtypeStruct((steps, 2 * count, lanes), jnp.bfloat16),
        compiler_params=pltpu.CompilerParams(vmem_limit_bytes=ROOM),
        cost_estimate=pl.CostEstimate(
            flops=2 * steps * 3 * count * 128 * lanes,
            bytes_accessed=4 * steps * count * lanes,
            transcendentals=0,
        ),
    )(order, ids, raw)


def mix_kernel(first, place_ref, *refs):
    out_ref = refs[-1]
    steps, count, _ = out_ref.shape
    for step in range(steps):
        part, total = first, None
        for ref in refs[:-1]:
            if len(ref.shape) == len(out_ref.shape):
                total = total + ref[step]
                continue
            cores, devices, slots, _, rows, strip = ref.shape
            span = devices * rows
            for slot in range(slots):
                arrived = jnp.concatenate(
                    [ref[core, :, slot, step].reshape(span, strip) for core in range(cores)], axis=1
                )
                piece = jnp.dot(
                    place_ref[step, :, part * span : (part + 1) * span],
                    arrived,
                    preferred_element_type=jnp.float32,
                )
                piece = piece[:count] + piece[count:]
                total = piece if total is None else total + piece
                part += 1
        out_ref[step] = total.astype(out_ref.dtype)


def swap(value, offset):
    high, low = lax.axis_size("zh"), lax.axis_size("zl")
    pairs = []
    for z in range(offset, high * low + offset, low):
        a, b = [(at % low) * high + at // low % high for at in (z, z + 1)]
        pairs += [(a, b), (b, a)]
    return lax.ppermute(value, ("zl", "zh"), pairs)


def along_y(expert_ids):
    own = expert_ids.transpose(0, 2, 1)
    size = lax.axis_size("y")
    ring = [own]
    for away in range(1, size):
        ring.append(lax.ppermute(own, "y", [((at + away) % size, at) for at in range(size)]))
    return jnp.stack(ring)


def per_device(master, first_moment, second_moment, gradient, tokens, expert_ids, router_scores):
    steps, token_count, depth = tokens.shape
    quarters = lax.axis_size("x")
    cores = lax.axis_size("core")
    owners = lax.axis_size("zh")
    ys = lax.axis_size("y")
    groups = cores * ys
    z_low, z_high = lax.axis_index("zl"), lax.axis_index("zh")
    y_at, x_at = lax.axis_index("y"), lax.axis_index("x")

    all_tokens = lax.all_gather(
        tokens.reshape(steps * token_count, depth), ("core", "y"), axis=0, tiled=True
    )
    near_ids = along_y(expert_ids)

    turn = jnp.where(z_low == 0, 1, -1)
    order = jnp.mod(jnp.stack([z_high, z_high - turn, z_high + turn, z_high + 2]), owners)
    names = quarters * (y_at * owners + order) + x_at
    here = jnp.stack([z_low, lax.axis_index("core"), y_at])
    where = jnp.concatenate([here, names]).astype(jnp.int32)

    new_master, *chunks = adam(master, first_moment, second_moment, gradient, cores)
    rows, width = master.shape[1:]
    part = width // (cores * CHUNKS)
    strip = width // (quarters * cores)
    chunks = [chunk.reshape(-1, rows, part) for chunk in chunks]

    def share_out(chunk):
        moved = lax.all_to_all(chunk, ("core", "x"), split_axis=0, concat_axis=0, tiled=True)
        return moved.reshape(-1, part)

    hold = lax.optimization_barrier
    first_chunk, near_ids = hold((chunks[0], near_ids))
    own_a = share_out(first_chunk)
    far_ids = lax.ppermute(near_ids, "core", [(0, 1), (1, 0)])
    own_a, all_ids = hold((own_a, jnp.stack([near_ids, far_ids])))
    a1_a, c1_a = swap(own_a, 0), swap(own_a, 1)
    own_b = share_out(chunks[1])
    a1_b, c1_b = swap(own_b, 0), swap(own_b, 1)
    placed = place_rows(
        order.astype(jnp.int32), expert_ids, router_scores, PARTS * quarters * ys * CAP
    )
    a1_a, c1_a = hold((a1_a, c1_a))
    a2_a, c2_a = swap(c1_a, 0), swap(a1_a, 1)
    a1_b, c1_b, placed = hold((a1_b, c1_b, placed))
    a2_b, c2_b = swap(c1_b, 0), swap(a1_b, 1)
    rows = pick_rows(where, all_ids, all_tokens, steps * token_count)
    a2_a, c2_a = hold((a2_a, c2_a))
    a3_a, c3_a = swap(c2_a, 0), swap(a2_a, 1)
    a2_b, c2_b, *rows = hold((a2_b, c2_b, *rows))
    a3_b, c3_b = swap(c2_b, 0), swap(a2_b, 1)
    count = groups * steps * CAP
    double = jax.ShapeDtypeStruct((groups, quarters, 2, steps * CAP, strip), jnp.bfloat16)
    single = jax.ShapeDtypeStruct((groups, quarters, 1, steps * CAP, strip), jnp.bfloat16)
    start = jax.ShapeDtypeStruct((CHUNKS, count, part), jnp.float32)

    def send_back(value):
        slots = value.shape[2]
        value = value.reshape(groups * quarters, slots * steps * CAP, strip)
        back = lax.all_to_all(value, ("core", "y", "x"), split_axis=0, concat_axis=0, tiled=True)
        return back.reshape(cores, ys * quarters, slots, steps, CAP, strip)

    early = [rows[0], rows[1], own_a, own_b, a1_a, a1_b, c2_a, c2_b, c1_a, c1_b]
    early = run(early_kernel, early, double)
    a3_a, c3_a = hold((a3_a, c3_a))
    z4_a = swap(c3_a, 0)
    a3_b, c3_b, early = hold((a3_b, c3_b, early))
    early = send_back(early)
    z4_b = swap(a3_b, 1)
    later = run(later_kernel, [rows[2], a2_a, a2_b, a3_a, a3_b], single)
    begun = run(begin_kernel, [rows[3], c3_a, c3_b], start)
    mixed_shape = (steps, token_count, cores * strip)
    half_mixed = jax.ShapeDtypeStruct(mixed_shape, jnp.float32)
    half_mixed = run(functools.partial(mix_kernel, 0), [placed, early], half_mixed)
    z4_a, z4_b, later, begun, half_mixed = hold((z4_a, z4_b, later, begun, half_mixed))
    final = send_back(run(last_kernel, [rows[3], z4_a, z4_b, begun, later], double))
    mixed = jax.ShapeDtypeStruct(mixed_shape, jnp.bfloat16)
    mixed = run(functools.partial(mix_kernel, 2), [placed, final, half_mixed], mixed)
    return (new_master, mixed)


def solution(mesh):
    grid = Mesh(mesh.devices.reshape(2, 2, 4, 4, 4), ("zl", "core", "y", "zh", "x"))
    owner, part, group = ("y", "zh"), ("zl", "core", "x"), ("zl", "core", "y", "zh")
    weights = P(owner, part, None)
    routed = P(None, group, None)
    return jax.shard_map(
        per_device,
        mesh=grid,
        in_specs=(weights,) * 4 + (routed,) * 3,
        out_specs=(weights, P(None, group, "x")),
        check_vma=False,
    )
```

```python
import functools

import jax
import jax.numpy as jnp
from jax import lax
from jax.experimental import pallas as pl
from jax.experimental.pallas import tpu as pltpu
from jax.sharding import Mesh, PartitionSpec as P

learn_rate = 0.01
decay_rate = 0.1
beta_one = 0.9
beta_two = 0.95
epsilon = 1e-08
correct_one = 1.0 - 0.9**4
correct_two = 1.0 - 0.95**4

CAP = 32
PARTS = 4
CHUNKS = 2
STRIP = 128
ROOM = 12 * 2**20
WIDE = 56 * 2**20
PICK = 44 * 2**20
SMALL = pl.CostEstimate(flops=1, bytes_accessed=1, transcendentals=0)


def adam_kernel(master_ref, first_ref, second_ref, gradient_ref, new_ref, *chunk_refs):
    grad_full = gradient_ref[0].astype(jnp.float32)
    new_first = beta_one * first_ref[0] + (1.0 - beta_one) * grad_full
    new_second = beta_two * second_ref[0] + (1.0 - beta_two) * grad_full * grad_full
    update = new_first / correct_one / (jnp.sqrt(new_second / correct_two) + epsilon)
    updated = master_ref[0] * (1.0 - learn_rate * decay_rate) - learn_rate * update
    new_ref[0] = updated
    lowered = updated.astype(jnp.bfloat16)
    cores, _, _, part = chunk_refs[0].shape
    at = 0
    for ref in chunk_refs:
        for start in range(0, part, STRIP):
            for core in range(cores):
                ref[core, 0, :, start : start + STRIP] = lowered[:, at : at + STRIP]
                at += STRIP


def adam(master, first_moment, second_moment, gradient, cores):
    experts, rows, width = master.shape
    part = width // (cores * CHUNKS)
    cut = rows
    whole = pl.BlockSpec((1, cut, width), lambda i, j: (i, j, 0))
    block = pl.BlockSpec((cores, 1, cut, part), lambda i, j: (0, i, j, 0))
    chunk = jax.ShapeDtypeStruct((cores, experts, rows, part), jnp.bfloat16)
    return pl.pallas_call(
        adam_kernel,
        grid=(experts, 1),
        in_specs=[whole] * 4,
        out_specs=[whole] + [block] * CHUNKS,
        out_shape=[jax.ShapeDtypeStruct(master.shape, jnp.float32)] + [chunk] * CHUNKS,
        compiler_params=pltpu.CompilerParams(vmem_limit_bytes=WIDE),
        cost_estimate=pl.CostEstimate(
            flops=16 * master.size, bytes_accessed=20 * master.size, transcendentals=master.size
        ),
    )(master, first_moment, second_moment, gradient)


def pick_kernel(where_ref, ids_ref, low_ref, high_ref, *out_refs):
    steps, _, count = ids_ref.shape[2:]
    half = low_ref.shape[1]
    earlier = lax.broadcasted_iota(jnp.int32, (count, count), 0)
    later = lax.broadcasted_iota(jnp.int32, (count, count), 1)
    before = jnp.where(earlier < later, 1.0, 0.0).astype(jnp.bfloat16)
    slot = lax.broadcasted_iota(jnp.int32, (CAP, count), 0).astype(jnp.float32)
    for step in range(steps):
        ids = ids_ref[0, 0, step]
        masks = []
        for part in range(PARTS):
            hit = jnp.where(ids == where_ref[3 + part], 1.0, 0.0)
            masks.append(jnp.max(hit, axis=0, keepdims=True))
        mask = jnp.concatenate(masks * 2, axis=0)
        place = jnp.dot(
            mask.astype(jnp.bfloat16), before, preferred_element_type=jnp.float32
        )
        chosen = [
            jnp.where(slot == place[part : part + 1], mask[part : part + 1], 0.0)
            for part in range(PARTS)
        ]
        chosen = jnp.concatenate(chosen, axis=0).astype(jnp.bfloat16)
        rows = slice(step * count, (step + 1) * count)
        for at, ref in ((0, low_ref), (half, high_ref)):
            picked = jnp.dot(chosen, ref[rows, :], preferred_element_type=jnp.float32)
            picked = picked.astype(jnp.bfloat16)
            for part in range(PARTS):
                out_refs[part][step * CAP : (step + 1) * CAP, at : at + half] = picked[
                    part * CAP : (part + 1) * CAP
                ]


def pick_rows(where, all_ids, all_tokens, group_rows):
    _, ys, steps, choices, count = all_ids.shape
    total, depth = all_tokens.shape
    half = depth // 2
    groups = total // group_rows
    return pl.pallas_call(
        pick_kernel,
        grid_spec=pltpu.PrefetchScalarGridSpec(
            num_scalar_prefetch=1,
            grid=(groups,),
            in_specs=[
                pl.BlockSpec(
                    (1, 1, steps, choices, count),
                    lambda i, w: ((i // ys + w[1]) % 2, (i % ys + ys - w[2]) % ys, 0, 0, 0),
                ),
                pl.BlockSpec((group_rows, half), lambda i, w: (i, w[0])),
                pl.BlockSpec((group_rows, half), lambda i, w: (i, 1 - w[0])),
            ],
            out_specs=[pl.BlockSpec((steps * CAP, depth), lambda i, w: (i, 0))] * PARTS,
        ),
        out_shape=[jax.ShapeDtypeStruct((groups * steps * CAP, depth), jnp.bfloat16)] * PARTS,
        compiler_params=pltpu.CompilerParams(vmem_limit_bytes=PICK),
        cost_estimate=pl.CostEstimate(
            flops=8 * total * 128 * depth, bytes_accessed=4 * total * depth, transcendentals=0
        ),
    )(where, all_ids, all_tokens, all_tokens)


def halves(rows_ref, even, odd):
    half = rows_ref.shape[1] // 2
    total = None
    for at, weight in ((0, even), (half, odd)):
        if weight is not None:
            rows = rows_ref[:, at : at + half]
            piece = jnp.dot(rows, weight[...], preferred_element_type=jnp.float32)
            total = piece if total is None else total + piece
    return total


def act(out_ref, slot, chunk, product):
    value = (product * jax.nn.sigmoid(product)).astype(out_ref.dtype)
    groups, _, _, rows, strip = out_ref.shape
    wide = value.shape[1] // strip
    for group in range(groups):
        for column in range(wide):
            out_ref[group, chunk * wide + column, slot] = value[
                group * rows : (group + 1) * rows, column * strip : (column + 1) * strip
            ]


def early_kernel(rows_0, rows_1, own_a, own_b, a1_a, a1_b, c2_a, c2_b, c1_a, c1_b, out_ref):
    for chunk, (even, odd) in enumerate(((own_a, a1_a), (own_b, a1_b))):
        act(out_ref, 0, chunk, halves(rows_0, even, odd))
    for chunk, (even, odd) in enumerate(((c2_a, c1_a), (c2_b, c1_b))):
        act(out_ref, 1, chunk, halves(rows_1, even, odd))


def later_kernel(rows_2, a2_a, a2_b, a3_a, a3_b, out_ref):
    for chunk, (even, odd) in enumerate(((a2_a, a3_a), (a2_b, a3_b))):
        act(out_ref, 0, chunk, halves(rows_2, even, odd))


def begin_kernel(rows_3, c3_a, c3_b, start_ref):
    for chunk, odd in enumerate((c3_a, c3_b)):
        start_ref[chunk] = halves(rows_3, None, odd)


def last_kernel(rows_3, z4_a, z4_b, start_ref, acted_ref, out_ref):
    out_ref[:, :, :1] = acted_ref[...]
    for chunk, even in enumerate((z4_a, z4_b)):
        act(out_ref, 1, chunk, start_ref[chunk] + halves(rows_3, even, None))


def run(body, operands, out_shape):
    spec = pl.BlockSpec(memory_space=pltpu.VMEM)
    return pl.pallas_call(
        body,
        in_specs=[spec] * len(operands),
        out_specs=spec,
        out_shape=out_shape,
        compiler_params=pltpu.CompilerParams(vmem_limit_bytes=ROOM),
        cost_estimate=SMALL,
    )(*operands)


def place_kernel(order_ref, ids_ref, raw_ref, out_ref):
    count, choices = ids_ref.shape[1:]
    lanes = out_ref.shape[2]
    names = 128
    ids = ids_ref[0]
    raw = raw_ref[0]
    shares = raw / jnp.sum(raw, axis=1, keepdims=True)
    name = lax.broadcasted_iota(jnp.int32, (count, names), 1)
    mask = jnp.zeros((count, names), jnp.float32)
    weight = jnp.zeros((count, names), jnp.float32)
    for choice in range(choices):
        hit = ids[:, choice : choice + 1] == name
        mask = mask + jnp.where(hit, 1.0, 0.0)
        weight = weight + jnp.where(hit, shares[:, choice : choice + 1], 0.0)
    row = lax.broadcasted_iota(jnp.int32, (count, count), 0)
    column = lax.broadcasted_iota(jnp.int32, (count, count), 1)
    before = jnp.where(column < row, 1.0, 0.0).astype(jnp.bfloat16)
    place = jnp.dot(before, mask.astype(jnp.bfloat16), preferred_element_type=jnp.float32)
    place = jnp.where(mask > 0.0, place, 255.0).astype(jnp.bfloat16)
    high = weight.astype(jnp.bfloat16)
    low = (weight - high.astype(jnp.float32)).astype(jnp.bfloat16)
    stacked = jnp.concatenate([place, high, low], axis=0)
    span = lanes // PARTS
    for part in range(PARTS):
        lane = lax.broadcasted_iota(jnp.int32, (names, span), 1)
        device = lane // CAP
        expert = (device // 4 * 4 + order_ref[part]) * 4 + device % 4
        spread = jnp.where(
            lax.broadcasted_iota(jnp.int32, (names, span), 0) == expert, 1.0, 0.0
        ).astype(jnp.bfloat16)
        wide = jnp.dot(stacked, spread, preferred_element_type=jnp.float32)
        slot = (lax.broadcasted_iota(jnp.int32, (count, span), 1) % CAP).astype(jnp.float32)
        here = wide[:count] == slot
        at = slice(part * span, (part + 1) * span)
        out_ref[0, :count, at] = jnp.where(here, wide[count : 2 * count], 0.0).astype(jnp.bfloat16)
        out_ref[0, count:, at] = jnp.where(here, wide[2 * count :], 0.0).astype(jnp.bfloat16)


def place_rows(order, ids, raw, lanes):
    steps, count, choices = ids.shape
    return pl.pallas_call(
        place_kernel,
        grid_spec=pltpu.PrefetchScalarGridSpec(
            num_scalar_prefetch=1,
            grid=(steps,),
            in_specs=[pl.BlockSpec((1, count, choices), lambda i, w: (i, 0, 0))] * 2,
            out_specs=pl.BlockSpec((1, 2 * count, lanes), lambda i, w: (i, 0, 0)),
        ),
        out_shape=jax.ShapeDtypeStruct((steps, 2 * count, lanes), jnp.bfloat16),
        compiler_params=pltpu.CompilerParams(vmem_limit_bytes=ROOM),
        cost_estimate=pl.CostEstimate(
            flops=2 * steps * 3 * count * 128 * lanes,
            bytes_accessed=4 * steps * count * lanes,
            transcendentals=0,
        ),
    )(order, ids, raw)


def mix_kernel(first, place_ref, *refs):
    out_ref = refs[-1]
    steps, count, _ = out_ref.shape
    for step in range(steps):
        part, total = first, None
        for ref in refs[:-1]:
            if len(ref.shape) == len(out_ref.shape):
                total = total + ref[step]
                continue
            cores, devices, slots, _, rows, strip = ref.shape
            span = devices * rows
            for slot in range(slots):
                arrived = jnp.concatenate(
                    [ref[core, :, slot, step].reshape(span, strip) for core in range(cores)], axis=1
                )
                piece = jnp.dot(
                    place_ref[step, :, part * span : (part + 1) * span],
                    arrived,
                    preferred_element_type=jnp.float32,
                )
                piece = piece[:count] + piece[count:]
                total = piece if total is None else total + piece
                part += 1
        out_ref[step] = total.astype(out_ref.dtype)


def swap(value, offset):
    high, low = lax.axis_size("zh"), lax.axis_size("zl")
    pairs = []
    for z in range(offset, high * low + offset, low):
        a, b = [(at % low) * high + at // low % high for at in (z, z + 1)]
        pairs += [(a, b), (b, a)]
    return lax.ppermute(value, ("zl", "zh"), pairs)


def along_y(expert_ids):
    own = expert_ids.transpose(0, 2, 1)
    size = lax.axis_size("y")
    ring = [own]
    for away in range(1, size):
        ring.append(lax.ppermute(own, "y", [((at + away) % size, at) for at in range(size)]))
    return jnp.stack(ring)


def per_device(master, first_moment, second_moment, gradient, tokens, expert_ids, router_scores):
    steps, token_count, depth = tokens.shape
    quarters = lax.axis_size("x")
    cores = lax.axis_size("core")
    owners = lax.axis_size("zh")
    ys = lax.axis_size("y")
    groups = cores * ys
    z_low, z_high = lax.axis_index("zl"), lax.axis_index("zh")
    y_at, x_at = lax.axis_index("y"), lax.axis_index("x")

    all_tokens = lax.all_gather(
        tokens.reshape(steps * token_count, depth), ("core", "y"), axis=0, tiled=True
    )
    near_ids = along_y(expert_ids)

    turn = jnp.where(z_low == 0, 1, -1)
    order = jnp.mod(jnp.stack([z_high, z_high - turn, z_high + turn, z_high + 2]), owners)
    names = quarters * (y_at * owners + order) + x_at
    here = jnp.stack([z_low, lax.axis_index("core"), y_at])
    where = jnp.concatenate([here, names]).astype(jnp.int32)

    new_master, *chunks = adam(master, first_moment, second_moment, gradient, cores)
    rows, width = master.shape[1:]
    part = width // (cores * CHUNKS)
    strip = width // (quarters * cores)
    chunks = [chunk.reshape(-1, rows, part) for chunk in chunks]

    def share_out(chunk):
        moved = lax.all_to_all(chunk, ("core", "x"), split_axis=0, concat_axis=0, tiled=True)
        return moved.reshape(-1, part)

    hold = lax.optimization_barrier
    first_chunk, near_ids = hold((chunks[0], near_ids))
    own_a = share_out(first_chunk)
    far_ids = lax.ppermute(near_ids, "core", [(0, 1), (1, 0)])
    own_a, all_ids = hold((own_a, jnp.stack([near_ids, far_ids])))
    a1_a, c1_a = swap(own_a, 0), swap(own_a, 1)
    own_b = share_out(chunks[1])
    a1_b, c1_b = swap(own_b, 0), swap(own_b, 1)
    placed = place_rows(
        order.astype(jnp.int32), expert_ids, router_scores, PARTS * quarters * ys * CAP
    )
    a1_a, c1_a = hold((a1_a, c1_a))
    a2_a, c2_a = swap(c1_a, 0), swap(a1_a, 1)
    a1_b, c1_b, placed = hold((a1_b, c1_b, placed))
    a2_b, c2_b = swap(c1_b, 0), swap(a1_b, 1)
    rows = pick_rows(where, all_ids, all_tokens, steps * token_count)
    a2_a, c2_a = hold((a2_a, c2_a))
    a3_a, c3_a = swap(c2_a, 0), swap(a2_a, 1)
    a2_b, c2_b, *rows = hold((a2_b, c2_b, *rows))
    a3_b, c3_b = swap(c2_b, 0), swap(a2_b, 1)
    count = groups * steps * CAP
    double = jax.ShapeDtypeStruct((groups, quarters, 2, steps * CAP, strip), jnp.bfloat16)
    single = jax.ShapeDtypeStruct((groups, quarters, 1, steps * CAP, strip), jnp.bfloat16)
    start = jax.ShapeDtypeStruct((CHUNKS, count, part), jnp.float32)

    def send_back(value):
        slots = value.shape[2]
        value = value.reshape(groups * quarters, slots * steps * CAP, strip)
        back = lax.all_to_all(value, ("core", "y", "x"), split_axis=0, concat_axis=0, tiled=True)
        return back.reshape(cores, ys * quarters, slots, steps, CAP, strip)

    early = [rows[0], rows[1], own_a, own_b, a1_a, a1_b, c2_a, c2_b, c1_a, c1_b]
    early = run(early_kernel, early, double)
    a3_a, c3_a = hold((a3_a, c3_a))
    z4_a = swap(c3_a, 0)
    a3_b, c3_b, acted = hold((a3_b, c3_b, early))
    early = send_back(early)
    z4_b = swap(a3_b, 1)
    later = run(later_kernel, [rows[2], a2_a, a2_b, a3_a, a3_b], single)
    begun = run(begin_kernel, [rows[3], c3_a, c3_b], start)
    mixed_shape = (steps, token_count, cores * strip)
    half_mixed = jax.ShapeDtypeStruct(mixed_shape, jnp.float32)
    half_mixed = run(functools.partial(mix_kernel, 0), [placed, early], half_mixed)
    z4_a, z4_b, later, begun = hold((z4_a, z4_b, later, begun))
    final = send_back(run(last_kernel, [rows[3], z4_a, z4_b, begun, later], double))
    mixed = jax.ShapeDtypeStruct(mixed_shape, jnp.bfloat16)
    mixed = run(functools.partial(mix_kernel, 2), [placed, final, half_mixed], mixed)
    return (new_master, mixed)


def solution(mesh):
    grid = Mesh(mesh.devices.reshape(2, 2, 4, 4, 4), ("zl", "core", "y", "zh", "x"))
    owner, part, group = ("y", "zh"), ("zl", "core", "x"), ("zl", "core", "y", "zh")
    weights = P(owner, part, None)
    routed = P(None, group, None)
    return jax.shard_map(
        per_device,
        mesh=grid,
        in_specs=(weights,) * 4 + (routed,) * 3,
        out_specs=(weights, P(None, group, "x")),
        check_vma=False,
    )
```

```python
import functools

import jax
import jax.numpy as jnp
from jax import lax
from jax.experimental import pallas as pl
from jax.experimental.pallas import tpu as pltpu
from jax.sharding import Mesh, PartitionSpec as P

learn_rate = 0.01
decay_rate = 0.1
beta_one = 0.9
beta_two = 0.95
epsilon = 1e-08
correct_one = 1.0 - 0.9**4
correct_two = 1.0 - 0.95**4

CAP = 32
PARTS = 4
CHUNKS = 2
STRIP = 128
ROOM = 12 * 2**20
WIDE = 56 * 2**20
PICK = 44 * 2**20
SMALL = pl.CostEstimate(flops=1, bytes_accessed=1, transcendentals=0)


def adam_kernel(master_ref, first_ref, second_ref, gradient_ref, new_ref, *chunk_refs):
    grad_full = gradient_ref[0].astype(jnp.float32)
    new_first = beta_one * first_ref[0] + (1.0 - beta_one) * grad_full
    new_second = beta_two * second_ref[0] + (1.0 - beta_two) * grad_full * grad_full
    update = new_first / correct_one / (jnp.sqrt(new_second / correct_two) + epsilon)
    updated = master_ref[0] * (1.0 - learn_rate * decay_rate) - learn_rate * update
    new_ref[0] = updated
    lowered = updated.astype(jnp.bfloat16)
    cores, _, _, part = chunk_refs[0].shape
    at = 0
    for ref in chunk_refs:
        for start in range(0, part, STRIP):
            for core in range(cores):
                ref[core, 0, :, start : start + STRIP] = lowered[:, at : at + STRIP]
                at += STRIP


def adam(master, first_moment, second_moment, gradient, cores):
    experts, rows, width = master.shape
    part = width // (cores * CHUNKS)
    cut = rows
    whole = pl.BlockSpec((1, cut, width), lambda i, j: (i, j, 0))
    block = pl.BlockSpec((cores, 1, cut, part), lambda i, j: (0, i, j, 0))
    chunk = jax.ShapeDtypeStruct((cores, experts, rows, part), jnp.bfloat16)
    return pl.pallas_call(
        adam_kernel,
        grid=(experts, 1),
        in_specs=[whole] * 4,
        out_specs=[whole] + [block] * CHUNKS,
        out_shape=[jax.ShapeDtypeStruct(master.shape, jnp.float32)] + [chunk] * CHUNKS,
        compiler_params=pltpu.CompilerParams(vmem_limit_bytes=WIDE),
        cost_estimate=pl.CostEstimate(
            flops=16 * master.size, bytes_accessed=20 * master.size, transcendentals=master.size
        ),
    )(master, first_moment, second_moment, gradient)


def pick_kernel(where_ref, ids_ref, low_ref, high_ref, *out_refs):
    steps, _, count = ids_ref.shape[2:]
    half = low_ref.shape[1]
    earlier = lax.broadcasted_iota(jnp.int32, (count, count), 0)
    later = lax.broadcasted_iota(jnp.int32, (count, count), 1)
    before = jnp.where(earlier < later, 1.0, 0.0).astype(jnp.bfloat16)
    slot = lax.broadcasted_iota(jnp.int32, (CAP, count), 0).astype(jnp.float32)
    for step in range(steps):
        ids = ids_ref[0, 0, step]
        masks = []
        for part in range(PARTS):
            hit = jnp.where(ids == where_ref[3 + part], 1.0, 0.0)
            masks.append(jnp.max(hit, axis=0, keepdims=True))
        mask = jnp.concatenate(masks * 2, axis=0)
        place = jnp.dot(
            mask.astype(jnp.bfloat16), before, preferred_element_type=jnp.float32
        )
        chosen = [
            jnp.where(slot == place[part : part + 1], mask[part : part + 1], 0.0)
            for part in range(PARTS)
        ]
        chosen = jnp.concatenate(chosen, axis=0).astype(jnp.bfloat16)
        rows = slice(step * count, (step + 1) * count)
        for at, ref in ((0, low_ref), (half, high_ref)):
            picked = jnp.dot(chosen, ref[rows, :], preferred_element_type=jnp.float32)
            picked = picked.astype(jnp.bfloat16)
            for part in range(PARTS):
                out_refs[part][step * CAP : (step + 1) * CAP, at : at + half] = picked[
                    part * CAP : (part + 1) * CAP
                ]


def pick_rows(where, all_ids, all_tokens, group_rows):
    _, ys, steps, choices, count = all_ids.shape
    total, depth = all_tokens.shape
    half = depth // 2
    groups = total // group_rows
    return pl.pallas_call(
        pick_kernel,
        grid_spec=pltpu.PrefetchScalarGridSpec(
            num_scalar_prefetch=1,
            grid=(groups,),
            in_specs=[
                pl.BlockSpec(
                    (1, 1, steps, choices, count),
                    lambda i, w: ((i // ys + w[1]) % 2, (i % ys + ys - w[2]) % ys, 0, 0, 0),
                ),
                pl.BlockSpec((group_rows, half), lambda i, w: (i, w[0])),
                pl.BlockSpec((group_rows, half), lambda i, w: (i, 1 - w[0])),
            ],
            out_specs=[pl.BlockSpec((steps * CAP, depth), lambda i, w: (i, 0))] * PARTS,
        ),
        out_shape=[jax.ShapeDtypeStruct((groups * steps * CAP, depth), jnp.bfloat16)] * PARTS,
        compiler_params=pltpu.CompilerParams(vmem_limit_bytes=PICK),
        cost_estimate=pl.CostEstimate(
            flops=8 * total * 128 * depth, bytes_accessed=4 * total * depth, transcendentals=0
        ),
    )(where, all_ids, all_tokens, all_tokens)


def halves(rows_ref, even, odd):
    half = rows_ref.shape[1] // 2
    total = None
    for at, weight in ((0, even), (half, odd)):
        if weight is not None:
            rows = rows_ref[:, at : at + half]
            piece = jnp.dot(rows, weight[...], preferred_element_type=jnp.float32)
            total = piece if total is None else total + piece
    return total


def act(out_ref, slot, chunk, product):
    value = (product * jax.nn.sigmoid(product)).astype(out_ref.dtype)
    groups, _, _, rows, strip = out_ref.shape
    wide = value.shape[1] // strip
    for group in range(groups):
        for column in range(wide):
            out_ref[group, chunk * wide + column, slot] = value[
                group * rows : (group + 1) * rows, column * strip : (column + 1) * strip
            ]


def early_kernel(rows_0, rows_1, own_a, own_b, a1_a, a1_b, c2_a, c2_b, c1_a, c1_b, out_ref):
    for chunk, (even, odd) in enumerate(((own_a, a1_a), (own_b, a1_b))):
        act(out_ref, 0, chunk, halves(rows_0, even, odd))
    for chunk, (even, odd) in enumerate(((c2_a, c1_a), (c2_b, c1_b))):
        act(out_ref, 1, chunk, halves(rows_1, even, odd))


def later_kernel(rows_2, a2_a, a2_b, a3_a, a3_b, out_ref):
    for chunk, (even, odd) in enumerate(((a2_a, a3_a), (a2_b, a3_b))):
        act(out_ref, 0, chunk, halves(rows_2, even, odd))


def begin_kernel(rows_3, c3_a, c3_b, start_ref):
    for chunk, odd in enumerate((c3_a, c3_b)):
        start_ref[chunk] = halves(rows_3, None, odd)


def last_kernel(rows_3, z4_a, z4_b, start_ref, acted_ref, out_ref):
    out_ref[:, :, :1] = acted_ref[...]
    for chunk, even in enumerate((z4_a, z4_b)):
        act(out_ref, 1, chunk, start_ref[chunk] + halves(rows_3, even, None))


def run(body, operands, out_shape):
    spec = pl.BlockSpec(memory_space=pltpu.VMEM)
    return pl.pallas_call(
        body,
        in_specs=[spec] * len(operands),
        out_specs=spec,
        out_shape=out_shape,
        compiler_params=pltpu.CompilerParams(vmem_limit_bytes=ROOM),
        cost_estimate=SMALL,
    )(*operands)


def place_kernel(order_ref, ids_ref, raw_ref, out_ref):
    count, choices = ids_ref.shape[1:]
    lanes = out_ref.shape[2]
    names = 128
    ids = ids_ref[0]
    raw = raw_ref[0]
    shares = raw / jnp.sum(raw, axis=1, keepdims=True)
    name = lax.broadcasted_iota(jnp.int32, (count, names), 1)
    mask = jnp.zeros((count, names), jnp.float32)
    weight = jnp.zeros((count, names), jnp.float32)
    for choice in range(choices):
        hit = ids[:, choice : choice + 1] == name
        mask = mask + jnp.where(hit, 1.0, 0.0)
        weight = weight + jnp.where(hit, shares[:, choice : choice + 1], 0.0)
    row = lax.broadcasted_iota(jnp.int32, (count, count), 0)
    column = lax.broadcasted_iota(jnp.int32, (count, count), 1)
    before = jnp.where(column < row, 1.0, 0.0).astype(jnp.bfloat16)
    place = jnp.dot(before, mask.astype(jnp.bfloat16), preferred_element_type=jnp.float32)
    place = jnp.where(mask > 0.0, place, 255.0).astype(jnp.bfloat16)
    high = weight.astype(jnp.bfloat16)
    low = (weight - high.astype(jnp.float32)).astype(jnp.bfloat16)
    stacked = jnp.concatenate([place, high, low], axis=0)
    span = lanes // PARTS
    for part in range(PARTS):
        lane = lax.broadcasted_iota(jnp.int32, (names, span), 1)
        device = lane // CAP
        expert = (device // 4 * 4 + order_ref[part]) * 4 + device % 4
        spread = jnp.where(
            lax.broadcasted_iota(jnp.int32, (names, span), 0) == expert, 1.0, 0.0
        ).astype(jnp.bfloat16)
        wide = jnp.dot(stacked, spread, preferred_element_type=jnp.float32)
        slot = (lax.broadcasted_iota(jnp.int32, (count, span), 1) % CAP).astype(jnp.float32)
        here = wide[:count] == slot
        at = slice(part * span, (part + 1) * span)
        out_ref[0, :count, at] = jnp.where(here, wide[count : 2 * count], 0.0).astype(jnp.bfloat16)
        out_ref[0, count:, at] = jnp.where(here, wide[2 * count :], 0.0).astype(jnp.bfloat16)


def place_rows(order, ids, raw, lanes):
    steps, count, choices = ids.shape
    return pl.pallas_call(
        place_kernel,
        grid_spec=pltpu.PrefetchScalarGridSpec(
            num_scalar_prefetch=1,
            grid=(steps,),
            in_specs=[pl.BlockSpec((1, count, choices), lambda i, w: (i, 0, 0))] * 2,
            out_specs=pl.BlockSpec((1, 2 * count, lanes), lambda i, w: (i, 0, 0)),
        ),
        out_shape=jax.ShapeDtypeStruct((steps, 2 * count, lanes), jnp.bfloat16),
        compiler_params=pltpu.CompilerParams(vmem_limit_bytes=ROOM),
        cost_estimate=pl.CostEstimate(
            flops=2 * steps * 3 * count * 128 * lanes,
            bytes_accessed=4 * steps * count * lanes,
            transcendentals=0,
        ),
    )(order, ids, raw)


def mix_kernel(first, place_ref, *refs):
    out_ref = refs[-1]
    steps, count, _ = out_ref.shape
    for step in range(steps):
        part, total = first, None
        for ref in refs[:-1]:
            if len(ref.shape) == len(out_ref.shape):
                total = total + ref[step]
                continue
            cores, devices, slots, _, rows, strip = ref.shape
            span = devices * rows
            for slot in range(slots):
                arrived = jnp.concatenate(
                    [ref[core, :, slot, step].reshape(span, strip) for core in range(cores)], axis=1
                )
                piece = jnp.dot(
                    place_ref[step, :, part * span : (part + 1) * span],
                    arrived,
                    preferred_element_type=jnp.float32,
                )
                piece = piece[:count] + piece[count:]
                total = piece if total is None else total + piece
                part += 1
        out_ref[step] = total.astype(out_ref.dtype)


def swap(value, offset):
    high, low = lax.axis_size("zh"), lax.axis_size("zl")
    pairs = []
    for z in range(offset, high * low + offset, low):
        a, b = [(at % low) * high + at // low % high for at in (z, z + 1)]
        pairs += [(a, b), (b, a)]
    return lax.ppermute(value, ("zl", "zh"), pairs)


def along_y(expert_ids):
    own = expert_ids.transpose(0, 2, 1)
    size = lax.axis_size("y")
    ring = [own]
    for away in range(1, size):
        ring.append(lax.ppermute(own, "y", [((at + away) % size, at) for at in range(size)]))
    return jnp.stack(ring)


def per_device(master, first_moment, second_moment, gradient, tokens, expert_ids, router_scores):
    steps, token_count, depth = tokens.shape
    quarters = lax.axis_size("x")
    cores = lax.axis_size("core")
    owners = lax.axis_size("zh")
    ys = lax.axis_size("y")
    groups = cores * ys
    z_low, z_high = lax.axis_index("zl"), lax.axis_index("zh")
    y_at, x_at = lax.axis_index("y"), lax.axis_index("x")

    all_tokens = lax.all_gather(
        tokens.reshape(steps * token_count, depth), ("core", "y"), axis=0, tiled=True
    )
    near_ids = along_y(expert_ids)

    turn = jnp.where(z_low == 0, 1, -1)
    order = jnp.mod(jnp.stack([z_high, z_high - turn, z_high + turn, z_high + 2]), owners)
    names = quarters * (y_at * owners + order) + x_at
    here = jnp.stack([z_low, lax.axis_index("core"), y_at])
    where = jnp.concatenate([here, names]).astype(jnp.int32)

    new_master, *chunks = adam(master, first_moment, second_moment, gradient, cores)
    rows, width = master.shape[1:]
    part = width // (cores * CHUNKS)
    strip = width // (quarters * cores)
    chunks = [chunk.reshape(-1, rows, part) for chunk in chunks]

    def share_out(chunk):
        moved = lax.all_to_all(chunk, ("core", "x"), split_axis=0, concat_axis=0, tiled=True)
        return moved.reshape(-1, part)

    hold = lax.optimization_barrier
    first_chunk, near_ids = hold((chunks[0], near_ids))
    own_a = share_out(first_chunk)
    far_ids = lax.ppermute(near_ids, "core", [(0, 1), (1, 0)])
    own_a, all_ids = hold((own_a, jnp.stack([near_ids, far_ids])))
    a1_a, c1_a = swap(own_a, 0), swap(own_a, 1)
    own_b = share_out(chunks[1])
    a1_b, c1_b = swap(own_b, 0), swap(own_b, 1)
    placed = place_rows(
        order.astype(jnp.int32), expert_ids, router_scores, PARTS * quarters * ys * CAP
    )
    a1_a, c1_a = hold((a1_a, c1_a))
    a2_a, c2_a = swap(c1_a, 0), swap(a1_a, 1)
    a1_b, c1_b, placed = hold((a1_b, c1_b, placed))
    a2_b, c2_b = swap(c1_b, 0), swap(a1_b, 1)
    rows = pick_rows(where, all_ids, all_tokens, steps * token_count)
    a2_a, c2_a = hold((a2_a, c2_a))
    a3_a, c3_a = swap(c2_a, 0), swap(a2_a, 1)
    a2_b, c2_b, *rows = hold((a2_b, c2_b, *rows))
    a3_b, c3_b = swap(c2_b, 0), swap(a2_b, 1)
    count = groups * steps * CAP
    double = jax.ShapeDtypeStruct((groups, quarters, 2, steps * CAP, strip), jnp.bfloat16)
    single = jax.ShapeDtypeStruct((groups, quarters, 1, steps * CAP, strip), jnp.bfloat16)
    start = jax.ShapeDtypeStruct((CHUNKS, count, part), jnp.float32)

    def send_back(value):
        slots = value.shape[2]
        value = value.reshape(groups * quarters, slots * steps * CAP, strip)
        back = lax.all_to_all(value, ("core", "y", "x"), split_axis=0, concat_axis=0, tiled=True)
        return back.reshape(cores, ys * quarters, slots, steps, CAP, strip)

    early = [rows[0], rows[1], own_a, own_b, a1_a, a1_b, c2_a, c2_b, c1_a, c1_b]
    early = run(early_kernel, early, double)
    a3_a, c3_a = hold((a3_a, c3_a))
    z4_a = swap(c3_a, 0)
    a3_b, c3_b, early = hold((a3_b, c3_b, early))
    early = send_back(early)
    z4_b = swap(a3_b, 1)
    later = run(later_kernel, [rows[2], a2_a, a2_b, a3_a, a3_b], single)
    begun = run(begin_kernel, [rows[3], c3_a, c3_b], start)
    mixed_shape = (steps, token_count, cores * strip)
    half_mixed = jax.ShapeDtypeStruct(mixed_shape, jnp.float32)
    half_mixed = run(functools.partial(mix_kernel, 0), [placed, early], half_mixed)
    z4_a, z4_b, later, begun = hold((z4_a, z4_b, later, begun))
    final = send_back(run(last_kernel, [rows[3], z4_a, z4_b, begun, later], double))
    mixed = jax.ShapeDtypeStruct(mixed_shape, jnp.bfloat16)
    mixed = run(functools.partial(mix_kernel, 2), [placed, final, half_mixed], mixed)
    return (new_master, mixed)


def solution(mesh):
    grid = Mesh(mesh.devices.reshape(2, 2, 4, 4, 4), ("zl", "core", "y", "zh", "x"))
    owner, part, group = ("y", "zh"), ("zl", "core", "x"), ("zl", "core", "y", "zh")
    weights = P(owner, part, None)
    routed = P(None, group, None)
    return jax.shard_map(
        per_device,
        mesh=grid,
        in_specs=(weights,) * 4 + (routed,) * 3,
        out_specs=(weights, P(None, group, "x")),
        check_vma=False,
    )
```

```python
import functools

import jax
import jax.numpy as jnp
from jax import lax
from jax.experimental import pallas as pl
from jax.experimental.pallas import tpu as pltpu
from jax.sharding import Mesh, PartitionSpec as P

learn_rate = 0.01
decay_rate = 0.1
beta_one = 0.9
beta_two = 0.95
epsilon = 1e-08
correct_one = 1.0 - 0.9**4
correct_two = 1.0 - 0.95**4

CAP = 32
PARTS = 4
CHUNKS = 2
STRIP = 128
ROOM = 12 * 2**20
WIDE = 56 * 2**20
PICK = 44 * 2**20
SMALL = pl.CostEstimate(flops=1, bytes_accessed=1, transcendentals=0)


def adam_kernel(master_ref, first_ref, second_ref, gradient_ref, new_ref, *chunk_refs):
    grad_full = gradient_ref[0].astype(jnp.float32)
    new_first = beta_one * first_ref[0] + (1.0 - beta_one) * grad_full
    new_second = beta_two * second_ref[0] + (1.0 - beta_two) * grad_full * grad_full
    scale = jnp.sqrt(new_second * (1.0 / correct_two)) + epsilon
    update = new_first * (learn_rate / correct_one) / scale
    updated = master_ref[0] * (1.0 - learn_rate * decay_rate) - update
    new_ref[0] = updated
    lowered = updated.astype(jnp.bfloat16)
    cores, _, _, part = chunk_refs[0].shape
    at = 0
    for ref in chunk_refs:
        for start in range(0, part, STRIP):
            for core in range(cores):
                ref[core, 0, :, start : start + STRIP] = lowered[:, at : at + STRIP]
                at += STRIP


def adam(master, first_moment, second_moment, gradient, cores):
    experts, rows, width = master.shape
    part = width // (cores * CHUNKS)
    cut = rows
    whole = pl.BlockSpec((1, cut, width), lambda i, j: (i, j, 0))
    block = pl.BlockSpec((cores, 1, cut, part), lambda i, j: (0, i, j, 0))
    chunk = jax.ShapeDtypeStruct((cores, experts, rows, part), jnp.bfloat16)
    return pl.pallas_call(
        adam_kernel,
        grid=(experts, 1),
        in_specs=[whole] * 4,
        out_specs=[whole] + [block] * CHUNKS,
        out_shape=[jax.ShapeDtypeStruct(master.shape, jnp.float32)] + [chunk] * CHUNKS,
        compiler_params=pltpu.CompilerParams(vmem_limit_bytes=WIDE),
        cost_estimate=pl.CostEstimate(
            flops=16 * master.size, bytes_accessed=20 * master.size, transcendentals=master.size
        ),
    )(master, first_moment, second_moment, gradient)


def pick_kernel(where_ref, ids_ref, low_ref, high_ref, *out_refs):
    steps, _, count = ids_ref.shape[2:]
    half = low_ref.shape[1]
    earlier = lax.broadcasted_iota(jnp.int32, (count, count), 0)
    later = lax.broadcasted_iota(jnp.int32, (count, count), 1)
    before = jnp.where(earlier < later, 1.0, 0.0).astype(jnp.bfloat16)
    slot = lax.broadcasted_iota(jnp.int32, (CAP, count), 0).astype(jnp.float32)
    for step in range(steps):
        ids = ids_ref[0, 0, step]
        masks = []
        for part in range(PARTS):
            hit = jnp.where(ids == where_ref[3 + part], 1.0, 0.0)
            masks.append(jnp.max(hit, axis=0, keepdims=True))
        mask = jnp.concatenate(masks * 2, axis=0)
        place = jnp.dot(
            mask.astype(jnp.bfloat16), before, preferred_element_type=jnp.float32
        )
        chosen = [
            jnp.where(slot == place[part : part + 1], mask[part : part + 1], 0.0)
            for part in range(PARTS)
        ]
        chosen = jnp.concatenate(chosen, axis=0).astype(jnp.bfloat16)
        rows = slice(step * count, (step + 1) * count)
        for at, ref in ((0, low_ref), (half, high_ref)):
            picked = jnp.dot(chosen, ref[rows, :], preferred_element_type=jnp.float32)
            picked = picked.astype(jnp.bfloat16)
            for part in range(PARTS):
                out_refs[part][step * CAP : (step + 1) * CAP, at : at + half] = picked[
                    part * CAP : (part + 1) * CAP
                ]


def pick_rows(where, all_ids, all_tokens, group_rows):
    _, ys, steps, choices, count = all_ids.shape
    total, depth = all_tokens.shape
    half = depth // 2
    groups = total // group_rows
    return pl.pallas_call(
        pick_kernel,
        grid_spec=pltpu.PrefetchScalarGridSpec(
            num_scalar_prefetch=1,
            grid=(groups,),
            in_specs=[
                pl.BlockSpec(
                    (1, 1, steps, choices, count),
                    lambda i, w: ((i // ys + w[1]) % 2, (i % ys + ys - w[2]) % ys, 0, 0, 0),
                ),
                pl.BlockSpec((group_rows, half), lambda i, w: (i, w[0])),
                pl.BlockSpec((group_rows, half), lambda i, w: (i, 1 - w[0])),
            ],
            out_specs=[pl.BlockSpec((steps * CAP, depth), lambda i, w: (i, 0))] * PARTS,
        ),
        out_shape=[jax.ShapeDtypeStruct((groups * steps * CAP, depth), jnp.bfloat16)] * PARTS,
        compiler_params=pltpu.CompilerParams(vmem_limit_bytes=PICK),
        cost_estimate=pl.CostEstimate(
            flops=8 * total * 128 * depth, bytes_accessed=4 * total * depth, transcendentals=0
        ),
    )(where, all_ids, all_tokens, all_tokens)


def halves(rows_ref, even, odd):
    half = rows_ref.shape[1] // 2
    total = None
    for at, weight in ((0, even), (half, odd)):
        if weight is not None:
            rows = rows_ref[:, at : at + half]
            piece = jnp.dot(rows, weight[...], preferred_element_type=jnp.float32)
            total = piece if total is None else total + piece
    return total


def act(out_ref, slot, chunk, product):
    value = (product * jax.nn.sigmoid(product)).astype(out_ref.dtype)
    groups, _, _, rows, strip = out_ref.shape
    wide = value.shape[1] // strip
    for group in range(groups):
        for column in range(wide):
            out_ref[group, chunk * wide + column, slot] = value[
                group * rows : (group + 1) * rows, column * strip : (column + 1) * strip
            ]


def early_kernel(rows_0, rows_1, own_a, own_b, a1_a, a1_b, c2_a, c2_b, c1_a, c1_b, out_ref):
    for chunk, (even, odd) in enumerate(((own_a, a1_a), (own_b, a1_b))):
        act(out_ref, 0, chunk, halves(rows_0, even, odd))
    for chunk, (even, odd) in enumerate(((c2_a, c1_a), (c2_b, c1_b))):
        act(out_ref, 1, chunk, halves(rows_1, even, odd))


def later_kernel(rows_2, a2_a, a2_b, a3_a, a3_b, out_ref):
    for chunk, (even, odd) in enumerate(((a2_a, a3_a), (a2_b, a3_b))):
        act(out_ref, 0, chunk, halves(rows_2, even, odd))


def begin_kernel(rows_3, c3_a, c3_b, start_ref):
    for chunk, odd in enumerate((c3_a, c3_b)):
        start_ref[chunk] = halves(rows_3, None, odd)


def last_kernel(rows_3, z4_a, z4_b, start_ref, acted_ref, out_ref):
    out_ref[:, :, :1] = acted_ref[...]
    for chunk, even in enumerate((z4_a, z4_b)):
        act(out_ref, 1, chunk, start_ref[chunk] + halves(rows_3, even, None))


def run(body, operands, out_shape):
    spec = pl.BlockSpec(memory_space=pltpu.VMEM)
    return pl.pallas_call(
        body,
        in_specs=[spec] * len(operands),
        out_specs=spec,
        out_shape=out_shape,
        compiler_params=pltpu.CompilerParams(vmem_limit_bytes=ROOM),
        cost_estimate=SMALL,
    )(*operands)


def place_kernel(order_ref, ids_ref, raw_ref, out_ref):
    count, choices = ids_ref.shape[1:]
    lanes = out_ref.shape[2]
    names = 128
    ids = ids_ref[0]
    raw = raw_ref[0]
    shares = raw / jnp.sum(raw, axis=1, keepdims=True)
    name = lax.broadcasted_iota(jnp.int32, (count, names), 1)
    mask = jnp.zeros((count, names), jnp.float32)
    weight = jnp.zeros((count, names), jnp.float32)
    for choice in range(choices):
        hit = ids[:, choice : choice + 1] == name
        mask = mask + jnp.where(hit, 1.0, 0.0)
        weight = weight + jnp.where(hit, shares[:, choice : choice + 1], 0.0)
    row = lax.broadcasted_iota(jnp.int32, (count, count), 0)
    column = lax.broadcasted_iota(jnp.int32, (count, count), 1)
    before = jnp.where(column < row, 1.0, 0.0).astype(jnp.bfloat16)
    place = jnp.dot(before, mask.astype(jnp.bfloat16), preferred_element_type=jnp.float32)
    place = jnp.where(mask > 0.0, place, 255.0).astype(jnp.bfloat16)
    high = weight.astype(jnp.bfloat16)
    low = (weight - high.astype(jnp.float32)).astype(jnp.bfloat16)
    stacked = jnp.concatenate([place, high, low], axis=0)
    span = lanes // PARTS
    for part in range(PARTS):
        lane = lax.broadcasted_iota(jnp.int32, (names, span), 1)
        device = lane // CAP
        expert = (device // 4 * 4 + order_ref[part]) * 4 + device % 4
        spread = jnp.where(
            lax.broadcasted_iota(jnp.int32, (names, span), 0) == expert, 1.0, 0.0
        ).astype(jnp.bfloat16)
        wide = jnp.dot(stacked, spread, preferred_element_type=jnp.float32)
        slot = (lax.broadcasted_iota(jnp.int32, (count, span), 1) % CAP).astype(jnp.float32)
        here = wide[:count] == slot
        at = slice(part * span, (part + 1) * span)
        out_ref[0, :count, at] = jnp.where(here, wide[count : 2 * count], 0.0).astype(jnp.bfloat16)
        out_ref[0, count:, at] = jnp.where(here, wide[2 * count :], 0.0).astype(jnp.bfloat16)


def place_rows(order, ids, raw, lanes):
    steps, count, choices = ids.shape
    return pl.pallas_call(
        place_kernel,
        grid_spec=pltpu.PrefetchScalarGridSpec(
            num_scalar_prefetch=1,
            grid=(steps,),
            in_specs=[pl.BlockSpec((1, count, choices), lambda i, w: (i, 0, 0))] * 2,
            out_specs=pl.BlockSpec((1, 2 * count, lanes), lambda i, w: (i, 0, 0)),
        ),
        out_shape=jax.ShapeDtypeStruct((steps, 2 * count, lanes), jnp.bfloat16),
        compiler_params=pltpu.CompilerParams(vmem_limit_bytes=ROOM),
        cost_estimate=pl.CostEstimate(
            flops=2 * steps * 3 * count * 128 * lanes,
            bytes_accessed=4 * steps * count * lanes,
            transcendentals=0,
        ),
    )(order, ids, raw)


def mix_kernel(first, place_ref, *refs):
    out_ref = refs[-1]
    steps, count, _ = out_ref.shape
    for step in range(steps):
        part, total = first, None
        for ref in refs[:-1]:
            if len(ref.shape) == len(out_ref.shape):
                total = total + ref[step]
                continue
            cores, devices, slots, _, rows, strip = ref.shape
            span = devices * rows
            for slot in range(slots):
                arrived = jnp.concatenate(
                    [ref[core, :, slot, step].reshape(span, strip) for core in range(cores)], axis=1
                )
                piece = jnp.dot(
                    place_ref[step, :, part * span : (part + 1) * span],
                    arrived,
                    preferred_element_type=jnp.float32,
                )
                piece = piece[:count] + piece[count:]
                total = piece if total is None else total + piece
                part += 1
        out_ref[step] = total.astype(out_ref.dtype)


def swap(value, offset):
    high, low = lax.axis_size("zh"), lax.axis_size("zl")
    pairs = []
    for z in range(offset, high * low + offset, low):
        a, b = [(at % low) * high + at // low % high for at in (z, z + 1)]
        pairs += [(a, b), (b, a)]
    return lax.ppermute(value, ("zl", "zh"), pairs)


def along_y(expert_ids):
    own = expert_ids.transpose(0, 2, 1)
    size = lax.axis_size("y")
    ring = [own]
    for away in range(1, size):
        ring.append(lax.ppermute(own, "y", [((at + away) % size, at) for at in range(size)]))
    return jnp.stack(ring)


def per_device(master, first_moment, second_moment, gradient, tokens, expert_ids, router_scores):
    steps, token_count, depth = tokens.shape
    quarters = lax.axis_size("x")
    cores = lax.axis_size("core")
    owners = lax.axis_size("zh")
    ys = lax.axis_size("y")
    groups = cores * ys
    z_low, z_high = lax.axis_index("zl"), lax.axis_index("zh")
    y_at, x_at = lax.axis_index("y"), lax.axis_index("x")

    all_tokens = lax.all_gather(
        tokens.reshape(steps * token_count, depth), ("core", "y"), axis=0, tiled=True
    )
    near_ids = along_y(expert_ids)

    turn = jnp.where(z_low == 0, 1, -1)
    order = jnp.mod(jnp.stack([z_high, z_high - turn, z_high + turn, z_high + 2]), owners)
    names = quarters * (y_at * owners + order) + x_at
    here = jnp.stack([z_low, lax.axis_index("core"), y_at])
    where = jnp.concatenate([here, names]).astype(jnp.int32)

    new_master, *chunks = adam(master, first_moment, second_moment, gradient, cores)
    rows, width = master.shape[1:]
    part = width // (cores * CHUNKS)
    strip = width // (quarters * cores)
    chunks = [chunk.reshape(-1, rows, part) for chunk in chunks]

    def share_out(chunk):
        moved = lax.all_to_all(chunk, ("core", "x"), split_axis=0, concat_axis=0, tiled=True)
        return moved.reshape(-1, part)

    hold = lax.optimization_barrier
    first_chunk, near_ids = hold((chunks[0], near_ids))
    own_a = share_out(first_chunk)
    far_ids = lax.ppermute(near_ids, "core", [(0, 1), (1, 0)])
    own_a, all_ids = hold((own_a, jnp.stack([near_ids, far_ids])))
    a1_a, c1_a = swap(own_a, 0), swap(own_a, 1)
    own_b = share_out(chunks[1])
    a1_b, c1_b = swap(own_b, 0), swap(own_b, 1)
    placed = place_rows(
        order.astype(jnp.int32), expert_ids, router_scores, PARTS * quarters * ys * CAP
    )
    a1_a, c1_a = hold((a1_a, c1_a))
    a2_a, c2_a = swap(c1_a, 0), swap(a1_a, 1)
    a1_b, c1_b, placed = hold((a1_b, c1_b, placed))
    a2_b, c2_b = swap(c1_b, 0), swap(a1_b, 1)
    rows = pick_rows(where, all_ids, all_tokens, steps * token_count)
    a2_a, c2_a = hold((a2_a, c2_a))
    a3_a, c3_a = swap(c2_a, 0), swap(a2_a, 1)
    a2_b, c2_b, *rows = hold((a2_b, c2_b, *rows))
    a3_b, c3_b = swap(c2_b, 0), swap(a2_b, 1)
    count = groups * steps * CAP
    double = jax.ShapeDtypeStruct((groups, quarters, 2, steps * CAP, strip), jnp.bfloat16)
    single = jax.ShapeDtypeStruct((groups, quarters, 1, steps * CAP, strip), jnp.bfloat16)
    start = jax.ShapeDtypeStruct((CHUNKS, count, part), jnp.float32)

    def send_back(value):
        slots = value.shape[2]
        value = value.reshape(groups * quarters, slots * steps * CAP, strip)
        back = lax.all_to_all(value, ("core", "y", "x"), split_axis=0, concat_axis=0, tiled=True)
        return back.reshape(cores, ys * quarters, slots, steps, CAP, strip)

    early = [rows[0], rows[1], own_a, own_b, a1_a, a1_b, c2_a, c2_b, c1_a, c1_b]
    early = run(early_kernel, early, double)
    a3_a, c3_a = hold((a3_a, c3_a))
    z4_a = swap(c3_a, 0)
    a3_b, c3_b, early = hold((a3_b, c3_b, early))
    early = send_back(early)
    z4_b = swap(a3_b, 1)
    later = run(later_kernel, [rows[2], a2_a, a2_b, a3_a, a3_b], single)
    begun = run(begin_kernel, [rows[3], c3_a, c3_b], start)
    mixed_shape = (steps, token_count, cores * strip)
    half_mixed = jax.ShapeDtypeStruct(mixed_shape, jnp.float32)
    half_mixed = run(functools.partial(mix_kernel, 0), [placed, early], half_mixed)
    z4_a, z4_b, later, begun = hold((z4_a, z4_b, later, begun))
    final = send_back(run(last_kernel, [rows[3], z4_a, z4_b, begun, later], double))
    mixed = jax.ShapeDtypeStruct(mixed_shape, jnp.bfloat16)
    mixed = run(functools.partial(mix_kernel, 2), [placed, final, half_mixed], mixed)
    return (new_master, mixed)


def solution(mesh):
    grid = Mesh(mesh.devices.reshape(2, 2, 4, 4, 4), ("zl", "core", "y", "zh", "x"))
    owner, part, group = ("y", "zh"), ("zl", "core", "x"), ("zl", "core", "y", "zh")
    weights = P(owner, part, None)
    routed = P(None, group, None)
    return jax.shard_map(
        per_device,
        mesh=grid,
        in_specs=(weights,) * 4 + (routed,) * 3,
        out_specs=(weights, P(None, group, "x")),
        check_vma=False,
    )
```

```python
import functools

import jax
import jax.numpy as jnp
from jax import lax
from jax.experimental import pallas as pl
from jax.experimental.pallas import tpu as pltpu
from jax.sharding import Mesh, PartitionSpec as P

learn_rate = 0.01
decay_rate = 0.1
beta_one = 0.9
beta_two = 0.95
epsilon = 1e-08
correct_one = 1.0 - 0.9**4
correct_two = 1.0 - 0.95**4

CAP = 32
PARTS = 4
STRIP = 128
ROOM = 20 * 2**20
WIDE = 56 * 2**20
SMALL = pl.CostEstimate(flops=1, bytes_accessed=1, transcendentals=0)


def adam_kernel(master_ref, first_ref, second_ref, gradient_ref, new_ref, block_ref):
    grad_full = gradient_ref[0].astype(jnp.float32)
    new_first = beta_one * first_ref[0] + (1.0 - beta_one) * grad_full
    new_second = beta_two * second_ref[0] + (1.0 - beta_two) * grad_full * grad_full
    update = new_first / correct_one / (jnp.sqrt(new_second / correct_two) + epsilon)
    updated = master_ref[0] * (1.0 - learn_rate * decay_rate) - learn_rate * update
    new_ref[0] = updated
    lowered = updated.astype(jnp.bfloat16)
    cores, _, _, part = block_ref.shape
    at = 0
    for start in range(0, part, STRIP):
        for core in range(cores):
            block_ref[core, 0, :, start : start + STRIP] = lowered[:, at : at + STRIP]
            at += STRIP


def adam(master, first_moment, second_moment, gradient, cores):
    experts, rows, width = master.shape
    part = width // cores
    whole = pl.BlockSpec((1, rows, width), lambda i: (i, 0, 0))
    block = pl.BlockSpec((cores, 1, rows, part), lambda i: (0, i, 0, 0))
    chunk = jax.ShapeDtypeStruct((cores, experts, rows, part), jnp.bfloat16)
    return pl.pallas_call(
        adam_kernel,
        grid=(experts,),
        in_specs=[whole] * 4,
        out_specs=[whole, block],
        out_shape=[jax.ShapeDtypeStruct(master.shape, jnp.float32)] + [chunk],
        compiler_params=pltpu.CompilerParams(vmem_limit_bytes=WIDE),
        cost_estimate=pl.CostEstimate(
            flops=16 * master.size, bytes_accessed=20 * master.size, transcendentals=master.size
        ),
    )(master, first_moment, second_moment, gradient)


def pick_kernel(where_ref, ids_ref, tokens_ref, out_ref):
    count = ids_ref.shape[2]
    ys, parts = out_ref.shape[:2]
    earlier = lax.broadcasted_iota(jnp.int32, (count, count), 0)
    later = lax.broadcasted_iota(jnp.int32, (count, count), 1)
    before = jnp.where(earlier < later, 1.0, 0.0).astype(jnp.bfloat16)
    slot = lax.broadcasted_iota(jnp.int32, (CAP, count), 0).astype(jnp.float32)
    ids = ids_ref[0]
    masks = []
    for at in range(ys * parts):
        hit = jnp.where(ids == where_ref[1 + at], 1.0, 0.0)
        masks.append(jnp.max(hit, axis=0, keepdims=True))
    mask = jnp.concatenate(masks, axis=0)
    place = jnp.dot(mask.astype(jnp.bfloat16), before, preferred_element_type=jnp.float32)
    chosen = [
        jnp.where(slot == place[at : at + 1], mask[at : at + 1], 0.0) for at in range(ys * parts)
    ]
    chosen = jnp.concatenate(chosen, axis=0).astype(jnp.bfloat16)
    picked = jnp.dot(chosen, tokens_ref[0], preferred_element_type=jnp.float32)
    picked = picked.astype(jnp.bfloat16)
    for y in range(ys):
        for part in range(parts):
            at = (y * parts + part) * CAP
            out_ref[y, part] = picked[at : at + CAP]


def pick_rows(where, ids, tokens, ys):
    steps, choices, count = ids.shape
    depth = tokens.shape[2]
    half = depth // 2
    out = jax.ShapeDtypeStruct((ys, PARTS, steps * CAP, depth), jnp.bfloat16)
    return pl.pallas_call(
        pick_kernel,
        grid_spec=pltpu.PrefetchScalarGridSpec(
            num_scalar_prefetch=1,
            grid=(steps, 2),
            in_specs=[
                pl.BlockSpec((1, choices, count), lambda i, j, w: (i, 0, 0)),
                pl.BlockSpec((1, count, half), lambda i, j, w: (i, 0, (j + w[0]) % 2)),
            ],
            out_specs=pl.BlockSpec((ys, PARTS, CAP, half), lambda i, j, w: (0, 0, i, j)),
        ),
        out_shape=out,
        compiler_params=pltpu.CompilerParams(vmem_limit_bytes=ROOM),
        cost_estimate=SMALL,
    )(where, ids, tokens)


def multiply(rows_ref, weights, at=0):
    sides, ys, count, _ = rows_ref.shape
    total = None
    for weight in weights:
        depth = weight.shape[0]
        rows = rows_ref[:, :, :, at : at + depth].reshape(sides * ys * count, depth)
        piece = jnp.dot(rows, weight[...], preferred_element_type=jnp.float32)
        total = piece if total is None else total + piece
        at += depth
    return total


def fetch(near, far, part, held, sems, slot=0):
    copies = []
    for side, ref in enumerate((near, far)):
        copy = pltpu.make_async_copy(ref.at[:, part], held.at[slot, side], sems.at[slot, side])
        copy.start()
        copies.append(copy)
    return copies


def wait(copies):
    for copy in copies:
        copy.wait()


def act(out_ref, places, slot, product):
    value = (product * jax.nn.sigmoid(product)).astype(out_ref.dtype)
    _, _, _, rows, strip = out_ref.shape
    for away, place in enumerate(places):
        for column in range(value.shape[1] // strip):
            out_ref[place, column, slot] = value[
                away * rows : (away + 1) * rows, column * strip : (column + 1) * strip
            ]


def around(core_ref, ys):
    return [lax.rem(core_ref[0] + side, 2) * ys + y for side in range(2) for y in range(ys)]


def early_kernel(core_ref, near, far, *refs):
    weights, (out_ref, held, sems) = refs[:-3], refs[-3:]
    first, second = [fetch(near, far, part, held, sems, part) for part in range(2)]
    places = around(core_ref, near.shape[0])
    wait(first)
    act(out_ref, places, 0, multiply(held.at[0], weights[:4]))
    wait(second)
    act(out_ref, places, 1, multiply(held.at[1], weights[4:]))


def later_kernel(core_ref, near, far, *refs):
    weights, (out_ref, held, sems) = refs[:-3], refs[-3:]
    wait(fetch(near, far, 2, held, sems))
    act(out_ref, around(core_ref, near.shape[0]), 0, multiply(held.at[0], weights))


def begin_kernel(core_ref, near, far, c3_a, c3_b, start_ref, held, sems):
    wait(fetch(near, far, 3, held, sems))
    start_ref[...] = multiply(held.at[0], [c3_a, c3_b], near.shape[3] // 2)


def last_kernel(core_ref, near, far, z4_a, z4_b, start_ref, acted_ref, out_ref, held, sems):
    copies = fetch(near, far, 3, held, sems)
    out_ref[:, :, :1] = acted_ref[...]
    wait(copies)
    product = start_ref[...] + multiply(held.at[0], [z4_a, z4_b])
    act(out_ref, around(core_ref, near.shape[0]), 1, product)


def run(body, operands, out_shape, rows=None, core=None, slots=1):
    spec = pl.BlockSpec(memory_space=pltpu.VMEM)
    in_specs = [spec] * len(operands)
    scratch = []
    if rows is not None:
        in_specs = [
            pl.BlockSpec(memory_space=pltpu.SMEM),
            pl.BlockSpec(memory_space=pl.ANY),
            pl.BlockSpec(memory_space=pl.ANY),
        ] + in_specs
        operands = [core, *rows, *operands]
        ys, _, count, depth = rows[0].shape
        scratch = [
            pltpu.VMEM((slots, 2, ys, count, depth), jnp.bfloat16),
            pltpu.SemaphoreType.DMA((slots, 2)),
        ]
    return pl.pallas_call(
        body,
        in_specs=in_specs,
        out_specs=spec,
        out_shape=out_shape,
        scratch_shapes=scratch,
        compiler_params=pltpu.CompilerParams(vmem_limit_bytes=ROOM),
        cost_estimate=SMALL,
    )(*operands)


def place_kernel(order_ref, ids_ref, raw_ref, out_ref):
    count, choices = ids_ref.shape[1:]
    lanes = out_ref.shape[2]
    names = 128
    ids = ids_ref[0]
    raw = raw_ref[0]
    shares = raw / jnp.sum(raw, axis=1, keepdims=True)
    name = lax.broadcasted_iota(jnp.int32, (count, names), 1)
    mask = jnp.zeros((count, names), jnp.float32)
    weight = jnp.zeros((count, names), jnp.float32)
    for choice in range(choices):
        hit = ids[:, choice : choice + 1] == name
        mask = mask + jnp.where(hit, 1.0, 0.0)
        weight = weight + jnp.where(hit, shares[:, choice : choice + 1], 0.0)
    row = lax.broadcasted_iota(jnp.int32, (count, count), 0)
    column = lax.broadcasted_iota(jnp.int32, (count, count), 1)
    before = jnp.where(column < row, 1.0, 0.0).astype(jnp.bfloat16)
    place = jnp.dot(before, mask.astype(jnp.bfloat16), preferred_element_type=jnp.float32)
    place = jnp.where(mask > 0.0, place, 255.0).astype(jnp.bfloat16)
    high = weight.astype(jnp.bfloat16)
    low = (weight - high.astype(jnp.float32)).astype(jnp.bfloat16)
    stacked = jnp.concatenate([place, high, low], axis=0)
    span = lanes // PARTS
    for part in range(PARTS):
        lane = lax.broadcasted_iota(jnp.int32, (names, span), 1)
        device = lane // CAP
        expert = (device // 4 * 4 + order_ref[part]) * 4 + device % 4
        spread = jnp.where(
            lax.broadcasted_iota(jnp.int32, (names, span), 0) == expert, 1.0, 0.0
        ).astype(jnp.bfloat16)
        wide = jnp.dot(stacked, spread, preferred_element_type=jnp.float32)
        slot = (lax.broadcasted_iota(jnp.int32, (count, span), 1) % CAP).astype(jnp.float32)
        here = wide[:count] == slot
        at = slice(part * span, (part + 1) * span)
        out_ref[0, :count, at] = jnp.where(here, wide[count : 2 * count], 0.0).astype(jnp.bfloat16)
        out_ref[0, count:, at] = jnp.where(here, wide[2 * count :], 0.0).astype(jnp.bfloat16)


def place_rows(order, ids, raw, lanes):
    steps, count, choices = ids.shape
    return pl.pallas_call(
        place_kernel,
        grid_spec=pltpu.PrefetchScalarGridSpec(
            num_scalar_prefetch=1,
            grid=(steps,),
            in_specs=[pl.BlockSpec((1, count, choices), lambda i, w: (i, 0, 0))] * 2,
            out_specs=pl.BlockSpec((1, 2 * count, lanes), lambda i, w: (i, 0, 0)),
        ),
        out_shape=jax.ShapeDtypeStruct((steps, 2 * count, lanes), jnp.bfloat16),
        compiler_params=pltpu.CompilerParams(vmem_limit_bytes=ROOM),
        cost_estimate=SMALL,
    )(order, ids, raw)


def mix_kernel(first, place_ref, *refs):
    out_ref = refs[-1]
    steps, count, _ = out_ref.shape
    for step in range(steps):
        part, total = first, None
        for ref in refs[:-1]:
            if len(ref.shape) == len(out_ref.shape):
                total = total + ref[step]
                continue
            cores, devices, slots, _, rows, strip = ref.shape
            span = devices * rows
            for slot in range(slots):
                arrived = jnp.concatenate(
                    [ref[core, :, slot, step].reshape(span, strip) for core in range(cores)], axis=1
                )
                piece = jnp.dot(
                    place_ref[step, :, part * span : (part + 1) * span],
                    arrived,
                    preferred_element_type=jnp.float32,
                )
                piece = piece[:count] + piece[count:]
                total = piece if total is None else total + piece
                part += 1
        out_ref[step] = total.astype(out_ref.dtype)


def swap(value, offset):
    high, low = lax.axis_size("zh"), lax.axis_size("zl")
    pairs = []
    for z in range(offset, high * low + offset, low):
        a, b = [(at % low) * high + at // low % high for at in (z, z + 1)]
        pairs += [(a, b), (b, a)]
    return lax.ppermute(value, ("zl", "zh"), pairs)


def swap_cores(value):
    return lax.ppermute(value, "core", [(0, 1), (1, 0)])


def per_device(master, first_moment, second_moment, gradient, tokens, expert_ids, router_scores):
    steps, token_count, depth = tokens.shape
    quarters = lax.axis_size("x")
    cores = lax.axis_size("core")
    owners = lax.axis_size("zh")
    ys = lax.axis_size("y")
    groups = cores * ys
    z_low, z_high = lax.axis_index("zl"), lax.axis_index("zh")
    x_at = lax.axis_index("x")

    turn = jnp.where(z_low == 0, 1, -1)
    order = jnp.mod(jnp.stack([z_high, z_high - turn, z_high + turn, z_high + 2]), owners)
    names = quarters * (jnp.arange(ys)[:, None] * owners + order[None, :]) + x_at
    where = jnp.concatenate([z_low[None], names.reshape(-1)]).astype(jnp.int32)
    order = order.astype(jnp.int32)
    core = lax.axis_index("core").reshape(1).astype(jnp.int32)

    new_master, blocks = adam(master, first_moment, second_moment, gradient, cores)
    rows, width = master.shape[1:]
    part = width // cores
    strip = width // (quarters * cores)

    hold = lax.optimization_barrier
    blocks, tokens = hold((blocks.reshape(-1, rows, part), tokens))
    own = lax.all_to_all(blocks, ("core", "x"), split_axis=0, concat_axis=0, tiled=True)
    picked = pick_rows(where, expert_ids.transpose(0, 2, 1), tokens, ys)
    own, picked = hold((own, picked))
    near = lax.all_to_all(picked, "y", split_axis=0, concat_axis=0, tiled=True)
    own = own.reshape(-1, part)
    cut = own.shape[0] // 2
    own_a, own_b = own[:cut], own[cut:]
    a1_a, c1_a = swap(own_a, 0), swap(own_a, 1)
    a1_b, c1_b = swap(own_b, 0), swap(own_b, 1)
    placed = place_rows(order, expert_ids, router_scores, PARTS * quarters * ys * CAP)
    a1_a, c1_a = hold((a1_a, c1_a))
    a2_a, c2_a = swap(c1_a, 0), swap(a1_a, 1)
    a1_b, c1_b, placed, used_1 = hold((a1_b, c1_b, placed, a1_a))
    a2_b, c2_b = swap(c1_b, 0), swap(a1_b, 1)
    a2_a, c2_a = hold((a2_a, c2_a))
    a3_a, c3_a = swap(c2_a, 0), swap(a2_a, 1)
    a2_b, c2_b, used_2, near = hold((a2_b, c2_b, a2_a, near))
    a3_b, c3_b = swap(c2_b, 0), swap(a2_b, 1)
    sides = (near, swap_cores(near))
    double = jax.ShapeDtypeStruct((groups, quarters, 2, steps * CAP, strip), jnp.bfloat16)
    single = jax.ShapeDtypeStruct((groups, quarters, 1, steps * CAP, strip), jnp.bfloat16)
    start = jax.ShapeDtypeStruct((groups * steps * CAP, part), jnp.float32)

    def send_back(value):
        slots = value.shape[2]
        value = value.reshape(groups * quarters, slots * steps * CAP, strip)
        back = lax.all_to_all(value, ("core", "y", "x"), split_axis=0, concat_axis=0, tiled=True)
        return back.reshape(cores, ys * quarters, slots, steps, CAP, strip)

    a3_a, c3_a, own_a = hold((a3_a, c3_a, own_a))
    early = [own_a, own_b, used_1, a1_b, c2_a, c2_b, c1_a, c1_b]
    early = run(early_kernel, early, double, sides, core, 2)
    z4_a = swap(c3_a, 0)
    early = send_back(early)
    a3_b, c3_b, used_3 = hold((a3_b, c3_b, a3_a))
    z4_b = swap(a3_b, 1)
    later = run(later_kernel, [used_2, a2_b, used_3, a3_b], single, sides, core)
    begun = run(begin_kernel, [c3_a, c3_b], start, sides, core)
    mixed_shape = (steps, token_count, cores * strip)
    half_mixed = jax.ShapeDtypeStruct(mixed_shape, jnp.float32)
    half_mixed = run(functools.partial(mix_kernel, 0), [placed, early], half_mixed)
    z4_a, z4_b, begun, later = hold((z4_a, z4_b, begun, later))
    final = send_back(run(last_kernel, [z4_a, z4_b, begun, later], double, sides, core))
    mixed = jax.ShapeDtypeStruct(mixed_shape, jnp.bfloat16)
    mixed = run(functools.partial(mix_kernel, 2), [placed, final, half_mixed], mixed)
    return (new_master, mixed)


def solution(mesh):
    grid = Mesh(mesh.devices.reshape(2, 2, 4, 4, 4), ("zl", "core", "y", "zh", "x"))
    owner, part, group = ("y", "zh"), ("zl", "core", "x"), ("zl", "core", "y", "zh")
    weights = P(owner, part, None)
    routed = P(None, group, None)
    return jax.shard_map(
        per_device,
        mesh=grid,
        in_specs=(weights,) * 4 + (routed,) * 3,
        out_specs=(weights, P(None, group, "x")),
        check_vma=False,
    )
```

```python
import functools

import jax
import jax.numpy as jnp
from jax import lax
from jax.experimental import pallas as pl
from jax.experimental.pallas import tpu as pltpu
from jax.sharding import Mesh, PartitionSpec as P

learn_rate = 0.01
decay_rate = 0.1
beta_one = 0.9
beta_two = 0.95
epsilon = 1e-08
correct_one = 1.0 - 0.9**4
correct_two = 1.0 - 0.95**4

CAP = 32
PARTS = 4
CHUNKS = 2
STRIP = 128
ROOM = 6 * 2**20
WIDE = 56 * 2**20
PICK = 44 * 2**20
SMALL = pl.CostEstimate(flops=1, bytes_accessed=1, transcendentals=0)


def adam_kernel(master_ref, first_ref, second_ref, gradient_ref, new_ref, *chunk_refs):
    grad_full = gradient_ref[0].astype(jnp.float32)
    new_first = beta_one * first_ref[0] + (1.0 - beta_one) * grad_full
    new_second = beta_two * second_ref[0] + (1.0 - beta_two) * grad_full * grad_full
    update = new_first / correct_one / (jnp.sqrt(new_second / correct_two) + epsilon)
    updated = master_ref[0] * (1.0 - learn_rate * decay_rate) - learn_rate * update
    new_ref[0] = updated
    lowered = updated.astype(jnp.bfloat16)
    cores, _, _, part = chunk_refs[0].shape
    at = 0
    for ref in chunk_refs:
        for start in range(0, part, STRIP):
            for core in range(cores):
                ref[core, 0, :, start : start + STRIP] = lowered[:, at : at + STRIP]
                at += STRIP


def adam(master, first_moment, second_moment, gradient, cores):
    experts, rows, width = master.shape
    part = width // (cores * CHUNKS)
    cut = rows
    whole = pl.BlockSpec((1, cut, width), lambda i, j: (i, j, 0))
    block = pl.BlockSpec((cores, 1, cut, part), lambda i, j: (0, i, j, 0))
    chunk = jax.ShapeDtypeStruct((cores, experts, rows, part), jnp.bfloat16)
    return pl.pallas_call(
        adam_kernel,
        grid=(experts, 1),
        in_specs=[whole] * 4,
        out_specs=[whole] + [block] * CHUNKS,
        out_shape=[jax.ShapeDtypeStruct(master.shape, jnp.float32)] + [chunk] * CHUNKS,
        compiler_params=pltpu.CompilerParams(vmem_limit_bytes=WIDE),
        cost_estimate=pl.CostEstimate(
            flops=16 * master.size, bytes_accessed=20 * master.size, transcendentals=master.size
        ),
    )(master, first_moment, second_moment, gradient)


def pick_kernel(where_ref, ids_ref, low_ref, high_ref, *out_refs):
    steps, _, count = ids_ref.shape[2:]
    half = low_ref.shape[1]
    earlier = lax.broadcasted_iota(jnp.int32, (count, count), 0)
    later = lax.broadcasted_iota(jnp.int32, (count, count), 1)
    before = jnp.where(earlier < later, 1.0, 0.0).astype(jnp.bfloat16)
    slot = lax.broadcasted_iota(jnp.int32, (CAP, count), 0).astype(jnp.float32)
    for step in range(steps):
        ids = ids_ref[0, 0, step]
        masks = []
        for part in range(PARTS):
            hit = jnp.where(ids == where_ref[3 + part], 1.0, 0.0)
            masks.append(jnp.max(hit, axis=0, keepdims=True))
        mask = jnp.concatenate(masks * 2, axis=0)
        place = jnp.dot(
            mask.astype(jnp.bfloat16), before, preferred_element_type=jnp.float32
        )
        chosen = [
            jnp.where(slot == place[part : part + 1], mask[part : part + 1], 0.0)
            for part in range(PARTS)
        ]
        chosen = jnp.concatenate(chosen, axis=0).astype(jnp.bfloat16)
        rows = slice(step * count, (step + 1) * count)
        for at, ref in ((0, low_ref), (half, high_ref)):
            picked = jnp.dot(chosen, ref[rows, :], preferred_element_type=jnp.float32)
            picked = picked.astype(jnp.bfloat16)
            for part in range(PARTS):
                out_refs[part][step * CAP : (step + 1) * CAP, at : at + half] = picked[
                    part * CAP : (part + 1) * CAP
                ]


def pick_rows(where, all_ids, all_tokens, group_rows):
    _, ys, steps, choices, count = all_ids.shape
    total, depth = all_tokens.shape
    half = depth // 2
    groups = total // group_rows
    return pl.pallas_call(
        pick_kernel,
        grid_spec=pltpu.PrefetchScalarGridSpec(
            num_scalar_prefetch=1,
            grid=(groups,),
            in_specs=[
                pl.BlockSpec(
                    (1, 1, steps, choices, count),
                    lambda i, w: ((i // ys + w[1]) % 2, (i % ys + ys - w[2]) % ys, 0, 0, 0),
                ),
                pl.BlockSpec((group_rows, half), lambda i, w: (i, w[0])),
                pl.BlockSpec((group_rows, half), lambda i, w: (i, 1 - w[0])),
            ],
            out_specs=[pl.BlockSpec((steps * CAP, depth), lambda i, w: (i, 0))] * PARTS,
        ),
        out_shape=[jax.ShapeDtypeStruct((groups * steps * CAP, depth), jnp.bfloat16)] * PARTS,
        compiler_params=pltpu.CompilerParams(vmem_limit_bytes=PICK),
        cost_estimate=pl.CostEstimate(
            flops=8 * total * 128 * depth, bytes_accessed=4 * total * depth, transcendentals=0
        ),
    )(where, all_ids, all_tokens, all_tokens)


def halves(rows_ref, even, odd):
    half = rows_ref.shape[1] // 2
    total = None
    for at, weight in ((0, even), (half, odd)):
        if weight is not None:
            rows = rows_ref[:, at : at + half]
            piece = jnp.dot(rows, weight[...], preferred_element_type=jnp.float32)
            total = piece if total is None else total + piece
    return total


def act(out_ref, slot, chunk, product):
    value = (product * jax.nn.sigmoid(product)).astype(out_ref.dtype)
    groups, _, _, rows, strip = out_ref.shape
    wide = value.shape[1] // strip
    for group in range(groups):
        for column in range(wide):
            out_ref[group, chunk * wide + column, slot] = value[
                group * rows : (group + 1) * rows, column * strip : (column + 1) * strip
            ]


def early_kernel(rows_0, rows_1, own_a, own_b, a1_a, a1_b, c2_a, c2_b, c1_a, c1_b, out_ref):
    for chunk, (even, odd) in enumerate(((own_a, a1_a), (own_b, a1_b))):
        act(out_ref, 0, chunk, halves(rows_0, even, odd))
    for chunk, (even, odd) in enumerate(((c2_a, c1_a), (c2_b, c1_b))):
        act(out_ref, 1, chunk, halves(rows_1, even, odd))


def later_kernel(rows_2, a2_a, a2_b, a3_a, a3_b, out_ref):
    for chunk, (even, odd) in enumerate(((a2_a, a3_a), (a2_b, a3_b))):
        act(out_ref, 0, chunk, halves(rows_2, even, odd))


def begin_kernel(rows_3, c3_a, c3_b, start_ref):
    for chunk, odd in enumerate((c3_a, c3_b)):
        start_ref[chunk] = halves(rows_3, None, odd)


def last_kernel(rows_3, z4_a, z4_b, start_ref, acted_ref, out_ref):
    out_ref[:, :, :1] = acted_ref[...]
    for chunk, even in enumerate((z4_a, z4_b)):
        act(out_ref, 1, chunk, start_ref[chunk] + halves(rows_3, even, None))


def run(body, operands, out_shape):
    spec = pl.BlockSpec(memory_space=pltpu.VMEM)
    return pl.pallas_call(
        body,
        in_specs=[spec] * len(operands),
        out_specs=spec,
        out_shape=out_shape,
        compiler_params=pltpu.CompilerParams(vmem_limit_bytes=ROOM),
        cost_estimate=SMALL,
    )(*operands)


def place_kernel(order_ref, ids_ref, raw_ref, out_ref):
    count, choices = ids_ref.shape[1:]
    lanes = out_ref.shape[2]
    names = 128
    ids = ids_ref[0]
    raw = raw_ref[0]
    shares = raw / jnp.sum(raw, axis=1, keepdims=True)
    name = lax.broadcasted_iota(jnp.int32, (count, names), 1)
    mask = jnp.zeros((count, names), jnp.float32)
    weight = jnp.zeros((count, names), jnp.float32)
    for choice in range(choices):
        hit = ids[:, choice : choice + 1] == name
        mask = mask + jnp.where(hit, 1.0, 0.0)
        weight = weight + jnp.where(hit, shares[:, choice : choice + 1], 0.0)
    row = lax.broadcasted_iota(jnp.int32, (count, count), 0)
    column = lax.broadcasted_iota(jnp.int32, (count, count), 1)
    before = jnp.where(column < row, 1.0, 0.0).astype(jnp.bfloat16)
    place = jnp.dot(before, mask.astype(jnp.bfloat16), preferred_element_type=jnp.float32)
    place = jnp.where(mask > 0.0, place, 255.0).astype(jnp.bfloat16)
    high = weight.astype(jnp.bfloat16)
    low = (weight - high.astype(jnp.float32)).astype(jnp.bfloat16)
    stacked = jnp.concatenate([place, high, low], axis=0)
    span = lanes // PARTS
    for part in range(PARTS):
        lane = lax.broadcasted_iota(jnp.int32, (names, span), 1)
        device = lane // CAP
        expert = (device // 4 * 4 + order_ref[part]) * 4 + device % 4
        spread = jnp.where(
            lax.broadcasted_iota(jnp.int32, (names, span), 0) == expert, 1.0, 0.0
        ).astype(jnp.bfloat16)
        wide = jnp.dot(stacked, spread, preferred_element_type=jnp.float32)
        slot = (lax.broadcasted_iota(jnp.int32, (count, span), 1) % CAP).astype(jnp.float32)
        here = wide[:count] == slot
        at = slice(part * span, (part + 1) * span)
        out_ref[0, :count, at] = jnp.where(here, wide[count : 2 * count], 0.0).astype(jnp.bfloat16)
        out_ref[0, count:, at] = jnp.where(here, wide[2 * count :], 0.0).astype(jnp.bfloat16)


def place_rows(order, ids, raw, lanes):
    steps, count, choices = ids.shape
    return pl.pallas_call(
        place_kernel,
        grid_spec=pltpu.PrefetchScalarGridSpec(
            num_scalar_prefetch=1,
            grid=(steps,),
            in_specs=[pl.BlockSpec((1, count, choices), lambda i, w: (i, 0, 0))] * 2,
            out_specs=pl.BlockSpec((1, 2 * count, lanes), lambda i, w: (i, 0, 0)),
        ),
        out_shape=jax.ShapeDtypeStruct((steps, 2 * count, lanes), jnp.bfloat16),
        compiler_params=pltpu.CompilerParams(vmem_limit_bytes=ROOM),
        cost_estimate=pl.CostEstimate(
            flops=2 * steps * 3 * count * 128 * lanes,
            bytes_accessed=4 * steps * count * lanes,
            transcendentals=0,
        ),
    )(order, ids, raw)


def mix_kernel(first, place_ref, *refs):
    out_ref = refs[-1]
    steps, count, _ = out_ref.shape
    for step in range(steps):
        part, total = first, None
        for ref in refs[:-1]:
            if len(ref.shape) == len(out_ref.shape):
                total = total + ref[step]
                continue
            cores, devices, slots, _, rows, strip = ref.shape
            span = devices * rows
            for slot in range(slots):
                arrived = jnp.concatenate(
                    [ref[core, :, slot, step].reshape(span, strip) for core in range(cores)], axis=1
                )
                piece = jnp.dot(
                    place_ref[step, :, part * span : (part + 1) * span],
                    arrived,
                    preferred_element_type=jnp.float32,
                )
                piece = piece[:count] + piece[count:]
                total = piece if total is None else total + piece
                part += 1
        out_ref[step] = total.astype(out_ref.dtype)


def swap(value, offset):
    high, low = lax.axis_size("zh"), lax.axis_size("zl")
    pairs = []
    for z in range(offset, high * low + offset, low):
        a, b = [(at % low) * high + at // low % high for at in (z, z + 1)]
        pairs += [(a, b), (b, a)]
    return lax.ppermute(value, ("zl", "zh"), pairs)


def along_y(expert_ids):
    own = expert_ids.transpose(0, 2, 1)
    size = lax.axis_size("y")
    ring = [own]
    for away in range(1, size):
        ring.append(lax.ppermute(own, "y", [((at + away) % size, at) for at in range(size)]))
    return jnp.stack(ring)


def per_device(master, first_moment, second_moment, gradient, tokens, expert_ids, router_scores):
    steps, token_count, depth = tokens.shape
    quarters = lax.axis_size("x")
    cores = lax.axis_size("core")
    owners = lax.axis_size("zh")
    ys = lax.axis_size("y")
    groups = cores * ys
    z_low, z_high = lax.axis_index("zl"), lax.axis_index("zh")
    y_at, x_at = lax.axis_index("y"), lax.axis_index("x")

    all_tokens = lax.all_gather(
        tokens.reshape(steps * token_count, depth), ("core", "y"), axis=0, tiled=True
    )
    near_ids = along_y(expert_ids)

    turn = jnp.where(z_low == 0, 1, -1)
    order = jnp.mod(jnp.stack([z_high, z_high - turn, z_high + turn, z_high + 2]), owners)
    names = quarters * (y_at * owners + order) + x_at
    here = jnp.stack([z_low, lax.axis_index("core"), y_at])
    where = jnp.concatenate([here, names]).astype(jnp.int32)

    new_master, *chunks = adam(master, first_moment, second_moment, gradient, cores)
    rows, width = master.shape[1:]
    part = width // (cores * CHUNKS)
    strip = width // (quarters * cores)
    chunks = [chunk.reshape(-1, rows, part) for chunk in chunks]

    def share_out(chunk):
        moved = lax.all_to_all(chunk, ("core", "x"), split_axis=0, concat_axis=0, tiled=True)
        return moved.reshape(-1, part)

    hold = lax.optimization_barrier
    first_chunk, near_ids = hold((chunks[0], near_ids))
    own_a = share_out(first_chunk)
    far_ids = lax.ppermute(near_ids, "core", [(0, 1), (1, 0)])
    own_a, all_ids = hold((own_a, jnp.stack([near_ids, far_ids])))
    a1_a, c1_a = swap(own_a, 0), swap(own_a, 1)
    own_b = share_out(chunks[1])
    a1_b, c1_b = swap(own_b, 0), swap(own_b, 1)
    placed = place_rows(
        order.astype(jnp.int32), expert_ids, router_scores, PARTS * quarters * ys * CAP
    )
    a1_a, c1_a = hold((a1_a, c1_a))
    a2_a, c2_a = swap(c1_a, 0), swap(a1_a, 1)
    a1_b, c1_b, placed = hold((a1_b, c1_b, placed))
    a2_b, c2_b = swap(c1_b, 0), swap(a1_b, 1)
    rows = pick_rows(where, all_ids, all_tokens, steps * token_count)
    a2_a, c2_a = hold((a2_a, c2_a))
    a3_a, c3_a = swap(c2_a, 0), swap(a2_a, 1)
    a2_b, c2_b, *rows = hold((a2_b, c2_b, *rows))
    a3_b, c3_b = swap(c2_b, 0), swap(a2_b, 1)
    count = groups * steps * CAP
    double = jax.ShapeDtypeStruct((groups, quarters, 2, steps * CAP, strip), jnp.bfloat16)
    single = jax.ShapeDtypeStruct((groups, quarters, 1, steps * CAP, strip), jnp.bfloat16)
    start = jax.ShapeDtypeStruct((CHUNKS, count, part), jnp.float32)

    def send_back(value):
        slots = value.shape[2]
        value = value.reshape(groups * quarters, slots * steps * CAP, strip)
        back = lax.all_to_all(value, ("core", "y", "x"), split_axis=0, concat_axis=0, tiled=True)
        return back.reshape(cores, ys * quarters, slots, steps, CAP, strip)

    early = [rows[0], rows[1], own_a, own_b, a1_a, a1_b, c2_a, c2_b, c1_a, c1_b]
    early = run(early_kernel, early, double)
    a3_a, c3_a = hold((a3_a, c3_a))
    z4_a = swap(c3_a, 0)
    a3_b, c3_b, early = hold((a3_b, c3_b, early))
    early = send_back(early)
    z4_b = swap(a3_b, 1)
    later = run(later_kernel, [rows[2], a2_a, a2_b, a3_a, a3_b], single)
    begun = run(begin_kernel, [rows[3], c3_a, c3_b], start)
    mixed_shape = (steps, token_count, cores * strip)
    half_mixed = jax.ShapeDtypeStruct(mixed_shape, jnp.float32)
    half_mixed = run(functools.partial(mix_kernel, 0), [placed, early], half_mixed)
    z4_a, z4_b, later, begun = hold((z4_a, z4_b, later, begun))
    final = send_back(run(last_kernel, [rows[3], z4_a, z4_b, begun, later], double))
    mixed = jax.ShapeDtypeStruct(mixed_shape, jnp.bfloat16)
    mixed = run(functools.partial(mix_kernel, 2), [placed, final, half_mixed], mixed)
    return (new_master, mixed)


def solution(mesh):
    grid = Mesh(mesh.devices.reshape(2, 2, 4, 4, 4), ("zl", "core", "y", "zh", "x"))
    owner, part, group = ("y", "zh"), ("zl", "core", "x"), ("zl", "core", "y", "zh")
    weights = P(owner, part, None)
    routed = P(None, group, None)
    return jax.shard_map(
        per_device,
        mesh=grid,
        in_specs=(weights,) * 4 + (routed,) * 3,
        out_specs=(weights, P(None, group, "x")),
        check_vma=False,
    )
```
